32 devices in a mesh: gz: 4 (over x, core), head: 2 (over y), tile: 4 (over z).
Axes of the slice: x: 2, y: 2, z: 4, core: 2. Of those that a mesh axis runs over, the one named last changes fastest.
Arguments:
- nodes_in: bfloat16 [131072, 256], P(('gz', 'tile')), may hold values from -6 to 6
- cotangent: bfloat16 [131072, 256], P(('gz', 'tile')), may hold values from -6 to 6
- w_query: bfloat16 [256, 256], P(None, 'head'), may hold values from -0.375 to 0.375
- w_key: bfloat16 [256, 256], P(None, 'head'), may hold values from -0.375 to 0.375
- w_value: bfloat16 [256, 256], P(None, 'head'), may hold values from -0.375 to 0.375
- w_out: bfloat16 [256, 256], P('head'), may hold values from -0.375 to 0.375
- counts: int32 [1024], replicated, may hold values from 4 to 128
Outputs:
- output: bfloat16 [131072, 256], P(('gz', 'tile'), 'head')
- grad_nodes: bfloat16 [131072, 256], P(('gz', 'tile'), 'head')
- grad_query: float32 [256, 256], P(None, 'head')
- grad_key: float32 [256, 256], P(None, 'head')
- grad_value: float32 [256, 256], P(None, 'head')
- grad_out: float32 [256, 256], P('head')
The draws below stay inside these ranges and needn't reach their ends.
Inputs may be any that keep to these rules, and one draw needn't show every extreme that they name: counts[b] is how many of the nodes b * 128 to (b + 1) * 128 - 1 are valid; the valid ones are the first of them.
All inputs are finite; a program needn't handle non-finite values.
Results may differ from the reference program's by a relative error of at most 0.012.
The reference program's roundings to bfloat16 on the way count: a program that leaves them out, or rounds other values in their place, can miss the bound.
Values may be sent and summed in bfloat16 or wider, within the bound.
A program may use at most 128 MiB of HBM per device.

```python
import math
import jax
import jax.numpy as jnp
import numpy as np
from jax import lax

C = 256
HEADS = 8
WINDOW = 128
HEAD_DIM = 32
HEADS_DEV = 4
NODES = 131072
N_HEAD = 2


def touch_ends(values, rng, low, top_value):
    longest = values.shape.index(max(values.shape))
    spots = []
    for shift in (0, 1):
        where = [jax.random.randint(jax.random.fold_in(rng, axis), (), 0, length) for axis, length in enumerate(values.shape)]
        where[longest] = (where[longest] + shift) % values.shape[longest]
        spots.append(tuple(where))
    return values.at[spots[0]].set(low).at[spots[1]].set(top_value)


def shard_levels(rng, extent, shards, least, top_value):
    factor_of, own = 1.0, jax.random.fold_in(rng, 6)
    for position, blocks in shards:
        heights = jnp.exp(jax.random.uniform(jax.random.fold_in(own, position), (blocks,), jnp.float32, least / len(shards), top_value / len(shards)))
        factor_of = factor_of * jnp.repeat(heights, extent[position] // blocks).reshape([-1 if axis == position else 1 for axis in range(len(extent))])
    return factor_of


def bell_draw(own_key, shape, deviation, reach, pieces=(), kind=jnp.bfloat16):
    values = deviation * jax.random.normal(own_key, shape, jnp.float32)
    if pieces:
        values = values * shard_levels(own_key, shape, pieces, -0.22, 0.18)
    return jnp.clip(values, -reach, reach).astype(kind)


def setup_inputs(seed: int = 0) -> dict:
    key_list = jax.random.split(jax.random.key(seed), 8)
    return {
        "nodes_in": bell_draw(key_list[0], (NODES, C), 1.0, 6.0, ((0, 16),)),
        "cotangent": bell_draw(key_list[1], (NODES, C), 1.0, 6.0, ((0, 16),)),
        "w_query": bell_draw(key_list[2], (C, C), C ** -0.5, 0.375, ((1, 2),)),
        "w_key": bell_draw(key_list[3], (C, C), C ** -0.5, 0.375, ((1, 2),)),
        "w_value": bell_draw(key_list[4], (C, C), C ** -0.5, 0.375, ((1, 2),)),
        "w_out": bell_draw(key_list[5], (C, C), C ** -0.5, 0.375, ((0, 2),)),
        "counts": touch_ends(jax.random.randint(key_list[6], (NODES // WINDOW,), 4, WINDOW + 1), jax.random.fold_in(key_list[6], 1), 4, WINDOW).astype(jnp.int32),
    }


def window_core(queries, key_block, values, valid_keys, dcontext, score_scale):
    scores = jnp.einsum("whqe,whke->whqk", queries.astype(jnp.float32), key_block.astype(jnp.float32)) * score_scale
    weights = jnp.exp(scores) * valid_keys[:, None, None, :]
    attention = weights / jnp.sum(weights, axis=-1, keepdims=True)
    attention_low = lax.optimization_barrier(attention.astype(jnp.bfloat16)).astype(jnp.float32)
    context = jnp.einsum("whqk,whke->whqe", attention_low, values.astype(jnp.float32)).astype(jnp.bfloat16)
    dattention = jnp.einsum("whqe,whke->whqk", dcontext.astype(jnp.float32), values.astype(jnp.float32))
    center = jnp.sum(attention * dattention, axis=-1, keepdims=True)
    dscores = lax.optimization_barrier((attention * (dattention - center)).astype(jnp.bfloat16)).astype(jnp.float32)
    dvalues = jnp.einsum("whqk,whqe->whke", attention_low, dcontext.astype(jnp.float32)).astype(jnp.bfloat16)
    dqueries = (score_scale * jnp.einsum("whqk,whke->whqe", dscores, key_block.astype(jnp.float32))).astype(jnp.bfloat16)
    key_grads = (score_scale * jnp.einsum("whqk,whqe->whke", dscores, queries.astype(jnp.float32))).astype(jnp.bfloat16)
    return context, dqueries, key_grads, dvalues


def to_windows(array, dilation):
    length, columns = array.shape
    head_count = columns // HEAD_DIM
    shaped = array.reshape(length // (WINDOW * dilation), WINDOW, dilation, head_count, HEAD_DIM)
    return shaped.transpose(0, 2, 3, 1, 4).reshape(-1, head_count, WINDOW, HEAD_DIM)


def mask_windows(valid_rows, dilation):
    length = valid_rows.shape[0]
    shaped = valid_rows.reshape(length // (WINDOW * dilation), WINDOW, dilation)
    return shaped.transpose(0, 2, 1).reshape(-1, WINDOW)


def from_windows(array, dilation, length):
    head_count = array.shape[1]
    shaped = array.reshape(length // (WINDOW * dilation), dilation, head_count, WINDOW, HEAD_DIM)
    return shaped.transpose(0, 3, 1, 2, 4).reshape(length, head_count * HEAD_DIM)


def dilated(queries, key_block, values, dcontext, valid, dilation):
    total = queries.shape[0]
    shift = (WINDOW // 2) * dilation
    score_scale = HEAD_DIM ** -0.5
    windowed = [to_windows(jnp.roll(array, -shift, axis=0), dilation) for array in (queries, key_block, values, dcontext)]
    valid_win = mask_windows(jnp.roll(valid, -shift, axis=0), dilation)
    window_count = valid_win.shape[0]
    block = math.gcd(64, window_count)

    def blocked(array):
        return array.reshape((window_count // block, block) + array.shape[1:])

    def per_block(group):
        return window_core(group[0], group[1], group[2], group[3], group[4], score_scale)

    stacked = (blocked(windowed[0]), blocked(windowed[1]), blocked(windowed[2]), blocked(valid_win), blocked(windowed[3]))
    results = lax.map(per_block, stacked)
    outputs = []
    for result in results:
        flat = result.reshape((window_count,) + result.shape[2:])
        outputs.append(jnp.roll(from_windows(flat, dilation, total), shift, axis=0))
    return outputs


def reference(nodes_in, cotangent, w_query, w_key, w_value, w_out, counts):
    total = nodes_in.shape[0]
    valid = (jnp.arange(WINDOW, dtype=jnp.int32)[None, :] < counts[:, None]).astype(jnp.float32).reshape(total)
    queries = jnp.dot(nodes_in, w_query, preferred_element_type=jnp.float32).astype(jnp.bfloat16)
    key_rows = jnp.dot(nodes_in, w_key, preferred_element_type=jnp.float32).astype(jnp.bfloat16)
    values = jnp.dot(nodes_in, w_value, preferred_element_type=jnp.float32).astype(jnp.bfloat16)
    masked_cot = cotangent * valid.astype(jnp.bfloat16)[:, None]
    dcontext = jnp.dot(masked_cot, w_out.T, preferred_element_type=jnp.float32).astype(jnp.bfloat16)
    per_device = HEADS_DEV
    near_heads = [head_id for head_id in range(HEADS) if head_id % per_device < per_device // 2]
    far_heads = [head_id for head_id in range(HEADS) if head_id % per_device >= per_device // 2]
    near_columns = np.concatenate([np.arange(head_id * HEAD_DIM, (head_id + 1) * HEAD_DIM) for head_id in near_heads])
    far_columns = np.concatenate([np.arange(head_id * HEAD_DIM, (head_id + 1) * HEAD_DIM) for head_id in far_heads])
    near_out = dilated(queries[:, near_columns], key_rows[:, near_columns], values[:, near_columns], dcontext[:, near_columns], valid, 1)
    far_out = dilated(queries[:, far_columns], key_rows[:, far_columns], values[:, far_columns], dcontext[:, far_columns], valid, 4)
    merged = []
    for near_part, far_part in zip(near_out, far_out):
        whole = jnp.zeros((total, C), jnp.bfloat16)
        merged.append(whole.at[:, near_columns].set(near_part).at[:, far_columns].set(far_part))
    context, dqueries, key_grads, dvalues = merged
    output = (valid[:, None] * jnp.dot(context, w_out, preferred_element_type=jnp.float32)).astype(jnp.bfloat16)
    group_width = C // N_HEAD
    summed = jnp.zeros((total, C), jnp.float32)
    for group in range(N_HEAD):
        low = group * group_width
        high = low + group_width
        partial_value = jnp.dot(dqueries[:, low:high], w_query[:, low:high].T, preferred_element_type=jnp.float32)
        partial_value = partial_value + jnp.dot(key_grads[:, low:high], w_key[:, low:high].T, preferred_element_type=jnp.float32)
        partial_value = partial_value + jnp.dot(dvalues[:, low:high], w_value[:, low:high].T, preferred_element_type=jnp.float32)
        summed = summed + lax.optimization_barrier(partial_value.astype(jnp.bfloat16)).astype(jnp.float32)
    grad_nodes = summed.astype(jnp.bfloat16)
    norm = float(total) ** -0.5
    grad_query = jnp.dot(nodes_in.T, dqueries, preferred_element_type=jnp.float32) * norm
    grad_key = jnp.dot(nodes_in.T, key_grads, preferred_element_type=jnp.float32) * norm
    grad_value = jnp.dot(nodes_in.T, dvalues, preferred_element_type=jnp.float32) * norm
    grad_out = jnp.dot(context.T, masked_cot, preferred_element_type=jnp.float32) * norm
    return (output, grad_nodes, grad_query, grad_key, grad_value, grad_out)
```

```python
import functools

import jax
import jax.numpy as jnp
from jax import lax
from jax.experimental import pallas as pl
from jax.experimental.pallas import tpu as pltpu
from jax.sharding import PartitionSpec as P

HEADS = 8
WINDOW = 128
DILATION = 4
TILE = WINDOW * DILATION
REACH = TILE // 2
LOW = jnp.bfloat16
NT = (((1,), (1,)), ((), ()))
TN = (((0,), (0,)), ((), ()))


def dot(a, b, dims=(((1,), (0,)), ((), ()))):
    return lax.dot_general(a, b, dims, preferred_element_type=jnp.float32)


def block_mask(count_of, rows, width):
    parts = []
    iota = lax.broadcasted_iota(jnp.int32, (WINDOW, width), 0)
    for block in range(rows // WINDOW):
        parts.append(jnp.where(iota < count_of(block), 1.0, 0.0))
    return jnp.concatenate(parts, 0)


def window_grads(q, k, v, dc, qt, kt, vt, dct, mask, scale, head_dim):
    heads = q.shape[1] // head_dim
    zeros = jnp.zeros((head_dim, WINDOW), LOW)
    lane = lax.broadcasted_iota(jnp.int32, q.shape, 1) // head_dim

    def spread_t(array):
        blocks = []
        for h in range(heads):
            rows = [zeros] * heads
            rows[h] = array[h * head_dim : (h + 1) * head_dim]
            blocks.append(jnp.concatenate(rows, 0))
        return jnp.concatenate(blocks, 1)

    def spread(array):
        return jnp.concatenate(
            [jnp.where(lane == h, array, jnp.zeros_like(array)) for h in range(heads)], 0
        )

    def pick(array):
        return jnp.concatenate(
            [
                array[h * head_dim : (h + 1) * head_dim, h * WINDOW : (h + 1) * WINDOW]
                for h in range(heads)
            ],
            0,
        )

    weights = jnp.exp(dot(k, spread_t(qt)) * scale) * mask
    attention = weights * (1.0 / jnp.sum(weights, axis=0, keepdims=True))
    attention_low = attention.astype(LOW)
    dattention = dot(v, spread_t(dct))
    center = jnp.sum(attention * dattention, axis=0, keepdims=True)
    dscores = (attention * (dattention - center)).astype(LOW)
    context = pick(dot(vt, attention_low)).astype(LOW).T
    dq = (pick(dot(kt, dscores)) * scale).astype(LOW).T
    dk = (dot(dscores, spread(q)) * scale).astype(LOW)
    dv = dot(attention_low, spread(dc)).astype(LOW)
    return jnp.concatenate([context, dq, dk, dv], 1)


def body(
    half, groups, head_dim, scale,
    counts, place,
    nodes, cot, halo, w_mine, w_peer,
    out_mine, grad_mine, out_peer, grad_peer, gw_mine, gw_peer,
    x_ext, c_ext, wt, perm, perm_t, near, far, gw, sems,
):
    first_block, h = place[0], place[1]
    width = nodes.shape[1]
    total_blocks = counts.shape[0]
    local_rows = half + REACH
    copies = []
    for index, (source, dest) in enumerate(((nodes, x_ext), (cot, c_ext))):
        src = pl.ds(pl.multiple_of(h * (half - REACH), REACH), local_rows)
        dst = pl.ds(pl.multiple_of((1 - h) * REACH, REACH), local_rows)
        copies.append(pltpu.make_async_copy(source.at[src], dest.at[dst], sems.at[2 * index]))
        rim = pl.ds(pl.multiple_of(h * local_rows, REACH), REACH)
        copies.append(
            pltpu.make_async_copy(
                halo.at[:, pl.ds(index * width, width)], dest.at[rim], sems.at[2 * index + 1]
            )
        )
    for copy in copies:
        copy.start()
    for part in range(2):
        for kind in range(4):
            for source, at in ((w_mine, 0), (w_peer, 64)):
                start = kind * 128 + part * 64
                wt[part * 4 + kind, at : at + 64, :] = source[start : start + 64, :]
    m = lax.broadcasted_iota(jnp.int32, (TILE, TILE), 0)
    n = lax.broadcasted_iota(jnp.int32, (TILE, TILE), 1)
    perm[...] = jnp.where(n == DILATION * (m % WINDOW) + m // WINDOW, 1.0, 0.0).astype(LOW)
    perm_t[...] = jnp.where(m == DILATION * (n % WINDOW) + n // WINDOW, 1.0, 0.0).astype(LOW)
    gw[...] = jnp.zeros_like(gw)
    tail = groups * TILE
    x_ext[tail:, :] = jnp.zeros((x_ext.shape[0] - tail, width), LOW)
    c_ext[tail:, :] = jnp.zeros((c_ext.shape[0] - tail, width), LOW)
    for copy in copies:
        copy.wait()

    def count_at(block):
        return counts[lax.rem(first_block + block + total_blocks, total_blocks)]

    def project(x, c, part):
        natural = [dot(a, wt[part * 4 + kind], NT).astype(LOW) for kind, a in enumerate((x, x, x, c))]
        turned = [dot(wt[part * 4 + kind], a, NT).astype(LOW) for kind, a in enumerate((x, x, x, c))]
        return natural, turned

    def windows(natural, turned, masks, store):
        for w in range(DILATION):
            rows = slice(w * WINDOW, (w + 1) * WINDOW)
            store(
                w,
                window_grads(
                    *[a[rows] for a in natural], *[a[:, rows] for a in turned],
                    masks[w], scale, head_dim,
                ),
            )

    iota = lax.broadcasted_iota(jnp.int32, (WINDOW, 4 * WINDOW), 0)

    def attend(g, carry):
        base = pl.multiple_of(g * TILE, TILE)
        block = g * DILATION
        c0 = [count_at(block + b) for b in range(DILATION + 1)]
        cot_mask = block_mask(lambda b: c0[b], TILE, width)
        cot_tile = (c_ext[pl.ds(base, TILE), :].astype(jnp.float32) * cot_mask).astype(LOW)
        edge = lax.broadcasted_iota(jnp.int32, (64, width), 0)
        after = c_ext[pl.ds(pl.multiple_of(base + TILE, TILE), 64), :].astype(jnp.float32)
        after = (after * jnp.where(edge < c0[DILATION], 1.0, 0.0)).astype(LOW)
        x_tile = x_ext[pl.ds(base, TILE), :]
        near_x = x_ext[pl.ds(pl.multiple_of(base + 64, 64), TILE), :]
        near_c = jnp.concatenate([cot_tile[64:], after], 0)
        masks = []
        for w in range(DILATION):
            masks.append(
                jnp.where(
                    iota < 64,
                    jnp.where(iota + 64 < c0[w], 1.0, 0.0),
                    jnp.where(iota - 64 < c0[w + 1], 1.0, 0.0),
                )
            )

        def store_near(w, value):
            near[pl.ds(pl.multiple_of(base + 64 + w * WINDOW, 64), WINDOW), :] = value

        windows(*project(near_x, near_c, 0), masks, store_near)

        far_x = dot(perm[...], x_tile).astype(LOW)
        far_c = dot(perm[...], cot_tile).astype(LOW)
        span = WINDOW // DILATION
        limit = jnp.where(
            iota < 2 * span,
            jnp.where(iota < span, c0[0], c0[1]),
            jnp.where(iota < 3 * span, c0[2], c0[3]),
        )
        spot = DILATION * (iota % span)
        masks = [jnp.where(spot + w < limit, 1.0, 0.0) for w in range(DILATION)]
        pieces = []
        windows(*project(far_x, far_c, 1), masks, lambda w, value: pieces.append(value))
        far[pl.ds(base, TILE), :] = dot(perm_t[...], jnp.concatenate(pieces, 0)).astype(LOW)
        return carry

    lax.fori_loop(0, groups, attend, 0)

    def finish(t, carry):
        base = pl.multiple_of(t * TILE + REACH, REACH)
        dest = pl.ds(pl.multiple_of(t * TILE, TILE), TILE)
        block = t * DILATION + REACH // WINDOW
        mask = block_mask(lambda b: count_at(block + b), TILE, width)
        x = x_ext[pl.ds(base, TILE), :]
        c = (c_ext[pl.ds(base, TILE), :].astype(jnp.float32) * mask).astype(LOW)
        res = [near[pl.ds(base, TILE), :], far[pl.ds(base, TILE), :]]
        out = sum(dot(res[p][:, :128], wt[p * 4 + 3]) for p in range(2)) * mask
        grad = sum(
            dot(res[p][:, 128 * (kind + 1) : 128 * (kind + 2)], wt[p * 4 + kind])
            for p in range(2)
            for kind in range(3)
        )
        for value, mine, peer in ((out, out_mine, out_peer), (grad, grad_mine, grad_peer)):
            value = value.astype(LOW)
            left, right = value[:, :128], value[:, 128:]
            mine[dest, :] = jnp.where(h == 0, left, right)
            peer[dest, :] = jnp.where(h == 0, right, left)
        xt, ct = x.T, c.T
        for p in range(2):
            gw[p, :, :128] += dot(ct, res[p][:, :128])
            gw[p, :, 128:] += dot(xt, res[p][:, 128:])
        return carry

    lax.fori_loop(0, half // TILE, finish, 0)
    for at, dest in ((0, gw_mine), (64, gw_peer)):
        for slot, kind in enumerate((1, 2, 3, 0)):
            start = kind * 128 + at
            dest[:, slot * 128 : (slot + 1) * 128] = jnp.concatenate(
                [gw[0, :, start : start + 64], gw[1, :, start : start + 64]], 1
            )


def per_device(nodes_in, cotangent, w_query, w_key, w_value, w_out, counts):
    row_count, width = nodes_in.shape
    half = row_count // 2
    head_dim = width // HEADS
    scale = head_dim ** (-0.5)
    h = lax.axis_index("head")
    places = lax.axis_size(("gz", "tile"))
    tiles = lax.axis_size("tile")
    position = lax.axis_index(("gz", "tile"))
    last = jnp.concatenate([nodes_in[row_count - REACH :], cotangent[row_count - REACH :]], 1)
    first = jnp.concatenate([nodes_in[:REACH], cotangent[:REACH]], 1)
    rim = jnp.where(h == 0, last, first)

    def index(place, head):
        return (place // tiles * 2 + head) * tiles + place % tiles

    route = [(index(p, 0), index((p + 1) % places, 0)) for p in range(places)]
    route += [(index(p, 1), index((p - 1) % places, 1)) for p in range(places)]
    halo = lax.ppermute(rim, ("gz", "head", "tile"), route)
    swap = [(0, 1), (1, 0)]
    w_mine = jnp.concatenate([w_query.T, w_key.T, w_value.T, w_out], 0)
    w_peer = lax.ppermute(w_mine, "head", swap)
    first_block = (position * row_count + h * half - REACH) // WINDOW
    place = jnp.stack([first_block, h]).astype(jnp.int32)
    groups = half // TILE + 1
    vmem = pl.BlockSpec(memory_space=pltpu.VMEM)
    smem = pl.BlockSpec(memory_space=pltpu.SMEM)
    anywhere = pl.BlockSpec(memory_space=pl.ANY)
    piece = jax.ShapeDtypeStruct((half, width // 2), LOW)
    sums = jax.ShapeDtypeStruct((width, 2 * width), jnp.float32)
    ext = groups * TILE + WINDOW
    out_mine, grad_mine, out_peer, grad_peer, gw_mine, gw_peer = pl.pallas_call(
        functools.partial(body, half, groups, head_dim, scale),
        out_shape=[piece] * 4 + [sums] * 2,
        in_specs=[smem, smem, anywhere, anywhere, anywhere, vmem, vmem],
        out_specs=[vmem] * 6,
        scratch_shapes=[
            pltpu.VMEM((ext, width), LOW),
            pltpu.VMEM((ext, width), LOW),
            pltpu.VMEM((8, width // 2, width), LOW),
            pltpu.VMEM((TILE, TILE), LOW),
            pltpu.VMEM((TILE, TILE), LOW),
            pltpu.VMEM((ext, 2 * width), LOW),
            pltpu.VMEM((ext, 2 * width), LOW),
            pltpu.VMEM((2, width, 2 * width), jnp.float32),
            pltpu.SemaphoreType.DMA((4,)),
        ],
        compiler_params=pltpu.CompilerParams(vmem_limit_bytes=56 * 1024 * 1024),
    )(counts, place, nodes_in, cotangent, halo, w_mine, w_peer)
    out_other = lax.ppermute(out_peer, "head", swap)
    grad_other = lax.ppermute(grad_peer, "head", swap)

    def merge(mine, other):
        return jnp.concatenate(
            [jnp.where(h == 0, mine, other), jnp.where(h == 0, other, mine)], 0
        )

    sums = gw_mine + lax.ppermute(gw_peer, "head", swap)
    sums = lax.psum(sums, ("gz", "tile")) * float(row_count * places) ** (-0.5)
    grad_query, grad_key, grad_value, grad_out = jnp.split(sums, 4, axis=1)
    return (
        merge(out_mine, out_other), merge(grad_mine, grad_other),
        grad_query, grad_key, grad_value, grad_out.T,
    )


def solution(mesh):
    return jax.shard_map(
        per_device,
        mesh=mesh,
        in_specs=(
            P(("gz", "tile"), None),
            P(("gz", "tile"), None),
            P(None, "head"),
            P(None, "head"),
            P(None, "head"),
            P("head", None),
            P(),
        ),
        out_specs=(
            P(("gz", "tile"), "head"),
            P(("gz", "tile"), "head"),
            P(None, "head"),
            P(None, "head"),
            P(None, "head"),
            P("head", None),
        ),
        check_vma=False,
    )
```

```python
import functools

import jax
import jax.numpy as jnp
from jax import lax
from jax.experimental import pallas as pl
from jax.experimental.pallas import tpu as pltpu
from jax.sharding import PartitionSpec as P

HEADS = 8
WINDOW = 128
DILATION = 4
TILE = WINDOW * DILATION
REACH = TILE // 2
LOW = jnp.bfloat16
NT = (((1,), (1,)), ((), ()))
MESH = pl.DeviceIdType.MESH


def dot(a, b, dims=(((1,), (0,)), ((), ()))):
    return lax.dot_general(a, b, dims, preferred_element_type=jnp.float32)


def block_mask(count_of, rows, width):
    parts = []
    iota = lax.broadcasted_iota(jnp.int32, (WINDOW, width), 0)
    for block in range(rows // WINDOW):
        parts.append(jnp.where(iota < count_of(block), 1.0, 0.0))
    return jnp.concatenate(parts, 0)


def window_grads(q, k, v, dc, qt, kt, vt, dct, mask, scale, head_dim):
    heads = q.shape[1] // head_dim
    zeros = jnp.zeros((head_dim, WINDOW), LOW)
    lane = lax.broadcasted_iota(jnp.int32, q.shape, 1) // head_dim

    def spread_t(array):
        blocks = []
        for h in range(heads):
            rows = [zeros] * heads
            rows[h] = array[h * head_dim : (h + 1) * head_dim]
            blocks.append(jnp.concatenate(rows, 0))
        return jnp.concatenate(blocks, 1)

    def spread(array):
        return jnp.concatenate(
            [jnp.where(lane == h, array, jnp.zeros_like(array)) for h in range(heads)], 0
        )

    def pick(array):
        return jnp.concatenate(
            [
                array[h * head_dim : (h + 1) * head_dim, h * WINDOW : (h + 1) * WINDOW]
                for h in range(heads)
            ],
            0,
        )

    weights = jnp.exp(dot(k, spread_t(qt)) * scale) * mask
    attention = weights * (1.0 / jnp.sum(weights, axis=0, keepdims=True))
    attention_low = attention.astype(LOW)
    dattention = dot(v, spread_t(dct))
    center = jnp.sum(attention * dattention, axis=0, keepdims=True)
    dscores = (attention * (dattention - center)).astype(LOW)
    context = pick(dot(vt, attention_low)).astype(LOW).T
    dq = (pick(dot(kt, dscores)) * scale).astype(LOW).T
    dk = (dot(dscores, spread(q)) * scale).astype(LOW)
    dv = dot(attention_low, spread(dc)).astype(LOW)
    return jnp.concatenate([context, dq, dk, dv], 1)


def body(
    half, groups, tiles, head_dim, scale,
    counts,
    nodes, cot, halo, w_mine, w_peer,
    out_all, grad_all, gw_all,
    x_ext, c_ext, wt, perm, perm_t, near, far, gw, mine_buf, peer_buf,
    sems, own_sems, send_sems, recv_sems,
):
    h = lax.axis_index("head")
    place = (lax.axis_index("gz") * tiles + lax.axis_index("tile")) * 2 + h
    first_block = place * (half // WINDOW) - REACH // WINDOW
    barrier = pltpu.get_barrier_semaphore()
    pl.semaphore_signal(barrier, inc=1, device_id={"head": 1 - h}, device_id_type=MESH)
    pl.semaphore_wait(barrier, 1)
    width = nodes.shape[1]
    total_blocks = counts.shape[0]
    local_rows = half + REACH
    copies = []
    for index, (source, dest) in enumerate(((nodes, x_ext), (cot, c_ext))):
        src = pl.ds(pl.multiple_of(h * (half - REACH), REACH), local_rows)
        dst = pl.ds(pl.multiple_of((1 - h) * REACH, REACH), local_rows)
        copies.append(pltpu.make_async_copy(source.at[src], dest.at[dst], sems.at[2 * index]))
        rim = pl.ds(pl.multiple_of(h * local_rows, REACH), REACH)
        copies.append(
            pltpu.make_async_copy(
                halo.at[:, pl.ds(index * width, width)], dest.at[rim], sems.at[2 * index + 1]
            )
        )
    for copy in copies:
        copy.start()
    for part in range(2):
        for kind in range(4):
            for source, at in ((w_mine, 0), (w_peer, 64)):
                start = kind * 128 + part * 64
                wt[part * 4 + kind, at : at + 64, :] = source[start : start + 64, :]
    m = lax.broadcasted_iota(jnp.int32, (TILE, TILE), 0)
    n = lax.broadcasted_iota(jnp.int32, (TILE, TILE), 1)
    perm[...] = jnp.where(n == DILATION * (m % WINDOW) + m // WINDOW, 1.0, 0.0).astype(LOW)
    perm_t[...] = jnp.where(m == DILATION * (n % WINDOW) + n // WINDOW, 1.0, 0.0).astype(LOW)
    gw[...] = jnp.zeros_like(gw)
    tail = groups * TILE
    x_ext[tail:, :] = jnp.zeros((x_ext.shape[0] - tail, width), LOW)
    c_ext[tail:, :] = jnp.zeros((c_ext.shape[0] - tail, width), LOW)
    for copy in copies:
        copy.wait()

    def count_at(block):
        return counts[lax.rem(first_block + block + total_blocks, total_blocks)]

    def project(x, c, part):
        natural = [dot(a, wt[part * 4 + kind], NT).astype(LOW) for kind, a in enumerate((x, x, x, c))]
        turned = [dot(wt[part * 4 + kind], a, NT).astype(LOW) for kind, a in enumerate((x, x, x, c))]
        return natural, turned

    def windows(natural, turned, masks, store):
        for w in range(DILATION):
            rows = slice(w * WINDOW, (w + 1) * WINDOW)
            store(
                w,
                window_grads(
                    *[a[rows] for a in natural], *[a[:, rows] for a in turned],
                    masks[w], scale, head_dim,
                ),
            )

    iota = lax.broadcasted_iota(jnp.int32, (WINDOW, 4 * WINDOW), 0)

    def attend(g):
        base = pl.multiple_of(g * TILE, TILE)
        block = g * DILATION
        c0 = [count_at(block + b) for b in range(DILATION + 1)]
        cot_mask = block_mask(lambda b: c0[b], TILE, width)
        cot_tile = (c_ext[pl.ds(base, TILE), :].astype(jnp.float32) * cot_mask).astype(LOW)
        edge = lax.broadcasted_iota(jnp.int32, (64, width), 0)
        after = c_ext[pl.ds(pl.multiple_of(base + TILE, TILE), 64), :].astype(jnp.float32)
        after = (after * jnp.where(edge < c0[DILATION], 1.0, 0.0)).astype(LOW)
        x_tile = x_ext[pl.ds(base, TILE), :]
        near_x = x_ext[pl.ds(pl.multiple_of(base + 64, 64), TILE), :]
        near_c = jnp.concatenate([cot_tile[64:], after], 0)
        masks = []
        for w in range(DILATION):
            masks.append(
                jnp.where(
                    iota < 64,
                    jnp.where(iota + 64 < c0[w], 1.0, 0.0),
                    jnp.where(iota - 64 < c0[w + 1], 1.0, 0.0),
                )
            )

        def store_near(w, value):
            near[pl.ds(pl.multiple_of(base + 64 + w * WINDOW, 64), WINDOW), :] = value

        windows(*project(near_x, near_c, 0), masks, store_near)

        far_x = dot(perm[...], x_tile).astype(LOW)
        far_c = dot(perm[...], cot_tile).astype(LOW)
        span = WINDOW // DILATION
        limit = jnp.where(
            iota < 2 * span,
            jnp.where(iota < span, c0[0], c0[1]),
            jnp.where(iota < 3 * span, c0[2], c0[3]),
        )
        spot = DILATION * (iota % span)
        masks = [jnp.where(spot + w < limit, 1.0, 0.0) for w in range(DILATION)]
        pieces = []
        windows(*project(far_x, far_c, 1), masks, lambda w, value: pieces.append(value))
        far[pl.ds(base, TILE), :] = dot(perm_t[...], jnp.concatenate(pieces, 0)).astype(LOW)

    def finish(t):
        base = pl.multiple_of(t * TILE + REACH, REACH)
        dest = pl.ds(pl.multiple_of(t * TILE, TILE), TILE)
        block = t * DILATION + REACH // WINDOW
        mask = block_mask(lambda b: count_at(block + b), TILE, width)
        x = x_ext[pl.ds(base, TILE), :]
        c = (c_ext[pl.ds(base, TILE), :].astype(jnp.float32) * mask).astype(LOW)
        res = [near[pl.ds(base, TILE), :], far[pl.ds(base, TILE), :]]
        out = sum(dot(res[p][:, :128], wt[p * 4 + 3]) for p in range(2)) * mask
        grad = sum(
            dot(res[p][:, 128 * (kind + 1) : 128 * (kind + 2)], wt[p * 4 + kind])
            for p in range(2)
            for kind in range(3)
        )
        home = pl.ds(pl.multiple_of(h * half + t * TILE, TILE), TILE)
        for slot, (value, whole) in enumerate(((out, out_all), (grad, grad_all))):
            value = value.astype(LOW)
            left, right = value[:, :128], value[:, 128:]
            mine_buf[slot, dest, :] = jnp.where(h == 0, left, right)
            peer_buf[slot, dest, :] = jnp.where(h == 0, right, left)
            pltpu.make_async_copy(
                mine_buf.at[slot, dest], whole.at[home], own_sems.at[slot]
            ).start()
            pltpu.make_async_remote_copy(
                src_ref=peer_buf.at[slot, dest],
                dst_ref=whole.at[home],
                send_sem=send_sems.at[slot],
                recv_sem=recv_sems.at[slot],
                device_id={"head": 1 - h},
                device_id_type=MESH,
            ).start()
        xt, ct = x.T, c.T
        for p in range(2):
            gw[p, :, :128] += dot(ct, res[p][:, :128])
            gw[p, :, 128:] += dot(xt, res[p][:, 128:])

    def step(g, carry):
        attend(g)

        @pl.when(g > 0)
        def _():
            finish(g - 1)

        return carry

    lax.fori_loop(0, groups, step, 0)
    for owner, at in ((0, 0), (1, 64)):
        for slot, kind in enumerate((1, 2, 3, 0)):
            start = kind * 128 + at
            gw_all[owner, :, slot * 128 : (slot + 1) * 128] = jnp.concatenate(
                [gw[0, :, start : start + 64], gw[1, :, start : start + 64]], 1
            )
    own_home = pl.ds(pl.multiple_of(h * half, TILE), half)
    peer_home = pl.ds(pl.multiple_of((1 - h) * half, TILE), half)
    for slot, whole in ((0, out_all), (1, grad_all)):
        pltpu.make_async_copy(mine_buf.at[slot], whole.at[own_home], own_sems.at[slot]).wait()
        sent = pltpu.make_async_remote_copy(
            src_ref=peer_buf.at[slot],
            dst_ref=whole.at[own_home],
            send_sem=send_sems.at[slot],
            recv_sem=recv_sems.at[slot],
            device_id={"head": 1 - h},
            device_id_type=MESH,
        )
        sent.wait_send()
        came = pltpu.make_async_remote_copy(
            src_ref=peer_buf.at[slot],
            dst_ref=whole.at[peer_home],
            send_sem=send_sems.at[slot],
            recv_sem=recv_sems.at[slot],
            device_id={"head": 1 - h},
            device_id_type=MESH,
        )
        came.wait_recv()


def reduce_body(
    places, tiles, norm, part, grad_query, grad_key, grad_value, grad_out,
    first, head_part, later, tile_part, summed, held, gathered, send_sems, recv_sems,
):
    gz, h, tile = lax.axis_index("gz"), lax.axis_index("head"), lax.axis_index("tile")
    bits = places.bit_length() - 1
    flags = [lax.rem(gz // (1 << k), 2) for k in range(bits)]
    partners = [{"gz": gz + (1 - 2 * flags[k]) * (1 << k)} for k in range(bits)]
    others = [{"tile": lax.rem(tile + d, tiles)} for d in range(1, tiles)]
    barrier = pltpu.get_barrier_semaphore()
    everyone = partners + [{"head": 1 - h}] + others
    for device in everyone:
        pl.semaphore_signal(barrier, inc=1, device_id=device, device_id_type=MESH)
    pl.semaphore_wait(barrier, len(everyone))
    used = [0]

    def send(source, dest, device):
        slot = used[0]
        used[0] += 1
        copy = pltpu.make_async_remote_copy(
            src_ref=source, dst_ref=dest, send_sem=send_sems.at[slot],
            recv_sem=recv_sems.at[slot], device_id=device, device_id_type=MESH,
        )
        copy.start()
        return copy

    rows, columns = part.shape[1:]
    size = rows // 2

    def keep(k):
        return pl.ds(pl.multiple_of(flags[k] * size, size), size)

    def give(k):
        return pl.ds(pl.multiple_of((1 - flags[k]) * size, size), size)

    send(part.at[:, give(0)], first, partners[0]).wait()
    summed[...] = part[1, keep(0), :] + first[1]
    copy = send(summed, head_part, {"head": 1 - h})
    held[:size, :] = part[0, keep(0), :] + first[0]
    copy.wait()
    held[:size, :] += head_part[...]
    base = flags[0] * size
    at = 0
    start = 0
    for k in range(1, bits):
        whole = size
        size = size // 2
        old = held.at[pl.ds(at, whole)]
        send(old.at[give(k)], later.at[pl.ds(start, size)], partners[k]).wait()
        at += whole
        held[at : at + size, :] = old[keep(k), :] + later[start : start + size, :]
        start += size
        base = base + flags[k] * size
    wide = columns // tiles

    def lanes(index):
        return pl.ds(pl.multiple_of(index * wide, wide), wide)

    current = held.at[pl.ds(at, size)]
    copies = [
        send(current.at[:, lanes(device["tile"])], tile_part.at[d], device)
        for d, device in enumerate(others)
    ]
    total = current[:, lanes(tile)]
    for d, copy in enumerate(copies):
        copy.wait()
        total = total + tile_part[d]
    mine = pl.ds(pl.multiple_of(base, size), size)
    gathered[mine, lanes(tile)] = (total * norm).astype(LOW)
    piece = gathered.at[mine, lanes(tile)]
    for copy in [send(piece, piece, device) for device in others]:
        copy.wait()
    for k in range(bits - 1, -1, -1):
        piece = gathered.at[pl.ds(pl.multiple_of(base, size), size)]
        send(piece, piece, partners[k]).wait()
        base = base - flags[k] * size
        size = size * 2
    result = gathered[...].astype(jnp.float32)
    quarter = columns // 4
    grad_query[...] = result[:, :quarter]
    grad_key[...] = result[:, quarter : 2 * quarter]
    grad_value[...] = result[:, 2 * quarter : 3 * quarter]
    grad_out[...] = result[:, 3 * quarter :].T


def reduce_sums(part, places, tiles, norm):
    rows, columns = part.shape[1:]
    bits = places.bit_length() - 1
    last = rows >> bits
    count = 2 * bits + 1 + 2 * (tiles - 1)
    vmem = pl.BlockSpec(memory_space=pltpu.VMEM)
    out = jax.ShapeDtypeStruct((rows, columns // 4), jnp.float32)
    return pl.pallas_call(
        functools.partial(reduce_body, places, tiles, norm),
        out_shape=[out] * 3 + [jax.ShapeDtypeStruct((columns // 4, rows), jnp.float32)],
        in_specs=[vmem],
        out_specs=[vmem] * 4,
        scratch_shapes=[
            pltpu.VMEM((2, rows // 2, columns), jnp.float32),
            pltpu.VMEM((rows // 2, columns), jnp.float32),
            pltpu.VMEM((rows // 2, columns), jnp.float32),
            pltpu.VMEM((tiles - 1, last, columns // tiles), jnp.float32),
            pltpu.VMEM((rows // 2, columns), jnp.float32),
            pltpu.VMEM((rows, columns), jnp.float32),
            pltpu.VMEM((rows, columns), LOW),
            pltpu.SemaphoreType.DMA((count,)),
            pltpu.SemaphoreType.DMA((count,)),
        ],
        compiler_params=pltpu.CompilerParams(
            vmem_limit_bytes=24 * 1024 * 1024, collective_id=1, has_side_effects=True
        ),
    )(part)


def per_device(nodes_in, cotangent, w_query, w_key, w_value, w_out, counts):
    row_count, width = nodes_in.shape
    half = row_count // 2
    head_dim = width // HEADS
    scale = head_dim ** (-0.5)
    h = lax.axis_index("head")
    places = lax.axis_size(("gz", "tile"))
    tiles = lax.axis_size("tile")
    last = jnp.concatenate([nodes_in[row_count - REACH :], cotangent[row_count - REACH :]], 1)
    first = jnp.concatenate([nodes_in[:REACH], cotangent[:REACH]], 1)
    rim = jnp.where(h == 0, last, first)

    def index(place, head):
        return (place // tiles * 2 + head) * tiles + place % tiles

    route = [(index(p, 0), index((p + 1) % places, 0)) for p in range(places)]
    route += [(index(p, 1), index((p - 1) % places, 1)) for p in range(places)]
    halo = lax.ppermute(rim, ("gz", "head", "tile"), route)
    swap = [(0, 1), (1, 0)]
    w_mine = jnp.concatenate([w_query.T, w_key.T, w_value.T, w_out], 0)
    w_peer = lax.ppermute(w_mine, "head", swap)
    groups = half // TILE + 1
    vmem = pl.BlockSpec(memory_space=pltpu.VMEM)
    smem = pl.BlockSpec(memory_space=pltpu.SMEM)
    anywhere = pl.BlockSpec(memory_space=pl.ANY)
    piece = jax.ShapeDtypeStruct((row_count, width // 2), LOW)
    sums = jax.ShapeDtypeStruct((2, width, 2 * width), jnp.float32)
    ext = groups * TILE + WINDOW
    output, grad_nodes, part = pl.pallas_call(
        functools.partial(body, half, groups, tiles, head_dim, scale),
        out_shape=[piece, piece, sums],
        in_specs=[smem, anywhere, anywhere, anywhere, vmem, vmem],
        out_specs=[anywhere, anywhere, vmem],
        scratch_shapes=[
            pltpu.VMEM((ext, width), LOW),
            pltpu.VMEM((ext, width), LOW),
            pltpu.VMEM((8, width // 2, width), LOW),
            pltpu.VMEM((TILE, TILE), LOW),
            pltpu.VMEM((TILE, TILE), LOW),
            pltpu.VMEM((ext, 2 * width), LOW),
            pltpu.VMEM((ext, 2 * width), LOW),
            pltpu.VMEM((2, width, 2 * width), jnp.float32),
            pltpu.VMEM((2, half, width // 2), LOW),
            pltpu.VMEM((2, half, width // 2), LOW),
            pltpu.SemaphoreType.DMA((4,)),
            pltpu.SemaphoreType.DMA((2,)),
            pltpu.SemaphoreType.DMA((2,)),
            pltpu.SemaphoreType.DMA((2,)),
        ],
        compiler_params=pltpu.CompilerParams(
            vmem_limit_bytes=56 * 1024 * 1024, collective_id=0, has_side_effects=True
        ),
    )(counts, nodes_in, cotangent, halo, w_mine, w_peer)
    norm = float(row_count * places) ** (-0.5)
    return (output, grad_nodes, *reduce_sums(part, lax.axis_size("gz"), tiles, norm))


def solution(mesh):
    return jax.shard_map(
        per_device,
        mesh=mesh,
        in_specs=(
            P(("gz", "tile"), None),
            P(("gz", "tile"), None),
            P(None, "head"),
            P(None, "head"),
            P(None, "head"),
            P("head", None),
            P(),
        ),
        out_specs=(
            P(("gz", "tile"), "head"),
            P(("gz", "tile"), "head"),
            P(None, "head"),
            P(None, "head"),
            P(None, "head"),
            P("head", None),
        ),
        check_vma=False,
    )
```

```python
import functools
import math

import jax
import jax.numpy as jnp
from jax import lax
from jax.experimental import pallas as pl
from jax.experimental.pallas import tpu as pltpu
from jax.sharding import PartitionSpec as P

HEADS = 8
WINDOW = 128
DILATION = 4
TILE = WINDOW * DILATION
REACH = TILE // 2
LOW = jnp.bfloat16
NT = (((1,), (1,)), ((), ()))
MESH = pl.DeviceIdType.MESH


def dot(a, b, dims=(((1,), (0,)), ((), ()))):
    return lax.dot_general(a, b, dims, preferred_element_type=jnp.float32)


def block_mask(count_of, rows, width):
    parts = []
    iota = lax.broadcasted_iota(jnp.int32, (WINDOW, width), 0)
    for block in range(rows // WINDOW):
        parts.append(jnp.where(iota < count_of(block), 1.0, 0.0))
    return jnp.concatenate(parts, 0)


def window_grads(q, k, v, dc, qt, kt, vt, dct, mask, scale, head_dim):
    heads = q.shape[1] // head_dim
    zeros = jnp.zeros((head_dim, WINDOW), LOW)
    lane = lax.broadcasted_iota(jnp.int32, q.shape, 1) // head_dim

    def spread_t(array):
        blocks = []
        for h in range(heads):
            rows = [zeros] * heads
            rows[h] = array[h * head_dim : (h + 1) * head_dim]
            blocks.append(jnp.concatenate(rows, 0))
        return jnp.concatenate(blocks, 1)

    def spread(array):
        return jnp.concatenate(
            [jnp.where(lane == h, array, jnp.zeros_like(array)) for h in range(heads)], 0
        )

    deep = heads // 2

    def pair_dot(turned, array):
        rows = deep * head_dim
        gap = jnp.zeros((rows, WINDOW), LOW)
        left = jnp.concatenate([turned[:rows], gap], 0)
        right = jnp.concatenate([gap, turned[rows:]], 0)
        stacked = jnp.concatenate([array[:, : deep * WINDOW], array[:, deep * WINDOW :]], 0)
        product = dot(jnp.concatenate([left, right], 1), stacked)
        return jnp.concatenate(
            [
                product[
                    h * head_dim : (h + 1) * head_dim,
                    (h % deep) * WINDOW : (h % deep + 1) * WINDOW,
                ]
                for h in range(heads)
            ],
            0,
        )

    weights = jnp.exp2(dot(k, spread_t(qt)) * (scale * math.log2(math.e))) * mask
    attention = weights * (1.0 / jnp.sum(weights, axis=0, keepdims=True))
    attention_low = attention.astype(LOW)
    dattention = dot(v, spread_t(dct))
    center = jnp.sum(attention * dattention, axis=0, keepdims=True)
    dscores = (attention * (dattention - center)).astype(LOW)
    context = pair_dot(vt, attention_low).astype(LOW).T
    dq = (pair_dot(kt, dscores) * scale).astype(LOW).T
    dk = (dot(dscores, spread(q)) * scale).astype(LOW)
    dv = dot(attention_low, spread(dc)).astype(LOW)
    return jnp.concatenate([context, dq, dk, dv], 1)


def body(
    half, groups, places, tiles, head_dim, scale, norm,
    counts, nodes, cot, w_query, w_key, w_value, w_out,
    out_all, grad_all, sums,
    x_ext, c_ext, wt, w_peer, wo_peer, perm, perm_t, near, far, gw, mine_buf, peer_buf,
    part, first, summed, head_a, head_b, later_a, later_b, sum_a, sum_b, held, later,
    tile_part, gathered, in_sems, own_sems, send_sems, recv_sems,
):
    gz, h, tile = lax.axis_index("gz"), lax.axis_index("head"), lax.axis_index("tile")
    position = gz * tiles + tile
    length = places * tiles
    first_block = (position * 2 + h) * (half // WINDOW) - REACH // WINDOW
    peer = {"head": 1 - h}
    bits = places.bit_length() - 1
    flags = [lax.rem(gz // (1 << k), 2) for k in range(bits)]
    partners = [{"gz": gz + (1 - 2 * flags[k]) * (1 << k)} for k in range(bits)]
    others = [{"tile": lax.rem(tile + d, tiles)} for d in range(1, tiles)]

    def along(distance):
        there = lax.rem(position + distance + length, length)
        return {"gz": there // tiles, "tile": lax.rem(there, tiles)}

    everyone = partners + [peer] + others + [along(1), along(-1)]
    barrier = pltpu.get_barrier_semaphore()
    for device in everyone:
        pl.semaphore_signal(barrier, inc=1, device_id=device, device_id_type=MESH)
    used = [2]

    def send(source, dest, device):
        slot = used[0]
        used[0] += 1
        copy = pltpu.make_async_remote_copy(
            src_ref=source, dst_ref=dest, send_sem=send_sems.at[slot],
            recv_sem=recv_sems.at[slot], device_id=device, device_id_type=MESH,
        )
        copy.start()
        return copy

    width = nodes.shape[1]
    total_blocks = counts.shape[0]
    local_rows = half + REACH
    copies = []
    for index, (source, dest) in enumerate(((nodes, x_ext), (cot, c_ext))):
        src = pl.ds(pl.multiple_of(h * (half - REACH), REACH), local_rows)
        dst = pl.ds(pl.multiple_of((1 - h) * REACH, REACH), local_rows)
        copies.append(pltpu.make_async_copy(source.at[src], dest.at[dst], in_sems.at[index]))
        copies[-1].start()
    pl.semaphore_wait(barrier, len(everyone))
    for index, source in enumerate((w_query, w_key, w_value)):
        copies.append(send(source, w_peer.at[index], peer))
    copies.append(send(w_out, wo_peer, peer))
    ahead = along(1 - 2 * h)
    edge_rows = pl.ds(pl.multiple_of((1 - h) * (2 * half - REACH), REACH), REACH)
    rim = pl.ds(pl.multiple_of(h * local_rows, REACH), REACH)
    for source, dest in ((nodes, x_ext), (cot, c_ext)):
        copies.append(send(source.at[edge_rows], dest.at[rim], ahead))

    def place_weight(kind, at, turned):
        for p in range(2):
            wt[p * 4 + kind, at : at + 64, :] = turned[p * 64 : (p + 1) * 64]

    for kind, source in enumerate((w_query, w_key, w_value)):
        place_weight(kind, 0, source[...].T)
    place_weight(3, 0, w_out[...])
    m = lax.broadcasted_iota(jnp.int32, (TILE, TILE), 0)
    n = lax.broadcasted_iota(jnp.int32, (TILE, TILE), 1)
    perm[...] = jnp.where(n == DILATION * (m % WINDOW) + m // WINDOW, 1.0, 0.0).astype(LOW)
    perm_t[...] = jnp.where(m == DILATION * (n % WINDOW) + n // WINDOW, 1.0, 0.0).astype(LOW)
    gw[...] = jnp.zeros_like(gw)
    tail = groups * TILE
    x_ext[tail:, :] = jnp.zeros((x_ext.shape[0] - tail, width), LOW)
    c_ext[tail:, :] = jnp.zeros((c_ext.shape[0] - tail, width), LOW)
    for copy in copies:
        copy.wait()
    for kind in range(3):
        place_weight(kind, 64, w_peer[kind].T)
    place_weight(3, 64, wo_peer[...])

    def count_at(block):
        return counts[lax.rem(first_block + block + total_blocks, total_blocks)]

    def project(x, c, part):
        natural = [dot(a, wt[part * 4 + kind], NT).astype(LOW) for kind, a in enumerate((x, x, x, c))]
        turned = [dot(wt[part * 4 + kind], a, NT).astype(LOW) for kind, a in enumerate((x, x, x, c))]
        return natural, turned

    def windows(natural, turned, masks, store):
        for w in range(DILATION):
            rows = slice(w * WINDOW, (w + 1) * WINDOW)
            store(
                w,
                window_grads(
                    *[a[rows] for a in natural], *[a[:, rows] for a in turned],
                    masks[w], scale, head_dim,
                ),
            )

    iota = lax.broadcasted_iota(jnp.int32, (WINDOW, 4 * WINDOW), 0)

    def attend(g):
        base = pl.multiple_of(g * TILE, TILE)
        block = g * DILATION
        c0 = [count_at(block + b) for b in range(DILATION + 1)]
        cot_mask = block_mask(lambda b: c0[b], TILE, width)
        cot_tile = (c_ext[pl.ds(base, TILE), :].astype(jnp.float32) * cot_mask).astype(LOW)
        edge = lax.broadcasted_iota(jnp.int32, (64, width), 0)
        after = c_ext[pl.ds(pl.multiple_of(base + TILE, TILE), 64), :].astype(jnp.float32)
        after = (after * jnp.where(edge < c0[DILATION], 1.0, 0.0)).astype(LOW)
        x_tile = x_ext[pl.ds(base, TILE), :]
        near_x = x_ext[pl.ds(pl.multiple_of(base + 64, 64), TILE), :]
        near_c = jnp.concatenate([cot_tile[64:], after], 0)
        masks = []
        for w in range(DILATION):
            masks.append(
                jnp.where(
                    iota < 64,
                    jnp.where(iota + 64 < c0[w], 1.0, 0.0),
                    jnp.where(iota - 64 < c0[w + 1], 1.0, 0.0),
                )
            )

        def store_near(w, value):
            near[pl.ds(pl.multiple_of(base + 64 + w * WINDOW, 64), WINDOW), :] = value

        windows(*project(near_x, near_c, 0), masks, store_near)

        far_x = dot(perm[...], x_tile).astype(LOW)
        far_c = dot(perm[...], cot_tile).astype(LOW)
        span = WINDOW // DILATION
        limit = jnp.where(
            iota < 2 * span,
            jnp.where(iota < span, c0[0], c0[1]),
            jnp.where(iota < 3 * span, c0[2], c0[3]),
        )
        spot = DILATION * (iota % span)
        masks = [jnp.where(spot + w < limit, 1.0, 0.0) for w in range(DILATION)]
        pieces = []
        windows(*project(far_x, far_c, 1), masks, lambda w, value: pieces.append(value))
        far[pl.ds(base, TILE), :] = dot(perm_t[...], jnp.concatenate(pieces, 0)).astype(LOW)

    def finish(t):
        base = pl.multiple_of(t * TILE + REACH, REACH)
        dest = pl.ds(pl.multiple_of(t * TILE, TILE), TILE)
        block = t * DILATION + REACH // WINDOW
        mask = block_mask(lambda b: count_at(block + b), TILE, width)
        x = x_ext[pl.ds(base, TILE), :]
        c = (c_ext[pl.ds(base, TILE), :].astype(jnp.float32) * mask).astype(LOW)
        res = [near[pl.ds(base, TILE), :], far[pl.ds(base, TILE), :]]
        out = sum(dot(res[p][:, :128], wt[p * 4 + 3]) for p in range(2)) * mask
        grad = sum(
            dot(res[p][:, 128 * (kind + 1) : 128 * (kind + 2)], wt[p * 4 + kind])
            for p in range(2)
            for kind in range(3)
        )
        home = pl.ds(pl.multiple_of(h * half + t * TILE, TILE), TILE)
        for slot, (value, whole) in enumerate(((out, out_all), (grad, grad_all))):
            value = value.astype(LOW)
            left, right = value[:, :128], value[:, 128:]
            mine_buf[slot, dest, :] = jnp.where(h == 0, left, right)
            peer_buf[slot, dest, :] = jnp.where(h == 0, right, left)
            pltpu.make_async_copy(
                mine_buf.at[slot, dest], whole.at[home], own_sems.at[slot]
            ).start()
            pltpu.make_async_remote_copy(
                src_ref=peer_buf.at[slot, dest],
                dst_ref=whole.at[home],
                send_sem=send_sems.at[slot],
                recv_sem=recv_sems.at[slot],
                device_id={"head": 1 - h},
                device_id_type=MESH,
            ).start()
        xt, ct = x.T, c.T
        for p in range(2):
            gw[p, :, :128] += dot(ct, res[p][:, :128])
            gw[p, :, 128:] += dot(xt, res[p][:, 128:])

    def step(g, carry):
        attend(g)

        @pl.when(g > 0)
        def _():
            finish(g - 1)

        return carry

    lax.fori_loop(0, groups, step, 0)
    for owner, at in ((0, 0), (1, 64)):
        for slot, kind in enumerate((1, 2, 3, 0)):
            start = kind * 128 + at
            part[owner, :, slot * 128 : (slot + 1) * 128] = jnp.concatenate(
                [gw[0, :, start : start + 64], gw[1, :, start : start + 64]], 1
            )
    rows, columns = part.shape[1:]
    middle = columns // 2
    size = rows // 2

    def keep(k):
        return pl.ds(pl.multiple_of(flags[k] * size, size), size)

    def give(k):
        return pl.ds(pl.multiple_of((1 - flags[k]) * size, size), size)

    send(part.at[:, give(0)], first, partners[0]).wait()
    summed[...] = part[:, keep(0), :] + first[...]
    base = flags[0] * size
    size = size // 2
    copy_a = send(summed.at[1, :, pl.ds(0, middle)], head_a, peer)
    copy_b = send(summed.at[:, give(1), pl.ds(middle, middle)], later_b, partners[1])
    copy_a.wait()
    sum_a[...] = summed[0, :, :middle] + head_a[...]
    copy_a = send(sum_a.at[give(1)], later_a, partners[1])
    copy_b.wait()
    sum_b[...] = summed[:, keep(1), middle:] + later_b[...]
    copy_b = send(sum_b.at[1], head_b, peer)
    copy_a.wait()
    copy_b.wait()
    held[:size, :middle] = sum_a[keep(1), :] + later_a[...]
    held[:size, middle:] = sum_b[0] + head_b[...]
    base = base + flags[1] * size
    at = 0
    start = 0
    for k in range(2, bits):
        whole = size
        size = size // 2
        old = held.at[pl.ds(at, whole)]
        send(old.at[give(k)], later.at[pl.ds(start, size)], partners[k]).wait()
        at += whole
        held[at : at + size, :] = old[keep(k), :] + later[start : start + size, :]
        start += size
        base = base + flags[k] * size
    wide = columns // tiles

    def lanes(index):
        return pl.ds(pl.multiple_of(index * wide, wide), wide)

    current = held.at[pl.ds(at, size)]
    copies = [
        send(current.at[:, lanes(device["tile"])], tile_part.at[d], device)
        for d, device in enumerate(others)
    ]
    total = current[:, lanes(tile)]
    for d, copy in enumerate(copies):
        copy.wait()
        total = total + tile_part[d]
    mine = pl.ds(pl.multiple_of(base, size), size)
    gathered[mine, lanes(tile)] = (total * norm).astype(LOW)
    piece = gathered.at[mine, lanes(tile)]
    for copy in [send(piece, piece, device) for device in others]:
        copy.wait()
    for k in range(bits - 1, -1, -1):
        piece = gathered.at[pl.ds(pl.multiple_of(base, size), size)]
        send(piece, piece, partners[k]).wait()
        base = base - flags[k] * size
        size = size * 2
    sums[...] = gathered[...]
    own_home = pl.ds(pl.multiple_of(h * half, TILE), half)
    peer_home = pl.ds(pl.multiple_of((1 - h) * half, TILE), half)
    for slot, whole in ((0, out_all), (1, grad_all)):
        pltpu.make_async_copy(mine_buf.at[slot], whole.at[own_home], own_sems.at[slot]).wait()
        sent = pltpu.make_async_remote_copy(
            src_ref=peer_buf.at[slot],
            dst_ref=whole.at[own_home],
            send_sem=send_sems.at[slot],
            recv_sem=recv_sems.at[slot],
            device_id={"head": 1 - h},
            device_id_type=MESH,
        )
        sent.wait_send()
        came = pltpu.make_async_remote_copy(
            src_ref=peer_buf.at[slot],
            dst_ref=whole.at[peer_home],
            send_sem=send_sems.at[slot],
            recv_sem=recv_sems.at[slot],
            device_id={"head": 1 - h},
            device_id_type=MESH,
        )
        came.wait_recv()


def hand_over(out_all, grad_all, sums, output, grad_nodes, *rest):
    grads, sems = rest[:4], rest[4]
    chunks = 4
    step = out_all.shape[0] // chunks
    copies = []
    for source, dest in ((out_all, output), (grad_all, grad_nodes)):
        for chunk in range(chunks):
            rows = pl.ds(chunk * step, step)
            copies.append(
                pltpu.make_async_copy(source.at[rows], dest.at[rows], sems.at[len(copies)])
            )
            copies[-1].start()
    result = sums[...].astype(jnp.float32)
    quarter = result.shape[1] // 4
    for slot in range(3):
        grads[slot][...] = result[:, slot * quarter : (slot + 1) * quarter]
    grads[3][...] = result[:, 3 * quarter :].T
    for copy in copies:
        copy.wait()


def per_device(nodes_in, cotangent, w_query, w_key, w_value, w_out, counts):
    row_count, width = nodes_in.shape
    half = row_count // 2
    head_dim = width // HEADS
    scale = head_dim ** (-0.5)
    places, tiles = lax.axis_size("gz"), lax.axis_size("tile")
    norm = float(row_count * places * tiles) ** (-0.5)
    groups = half // TILE + 1
    vmem = pl.BlockSpec(memory_space=pltpu.VMEM)
    smem = pl.BlockSpec(memory_space=pltpu.SMEM)
    anywhere = pl.BlockSpec(memory_space=pl.ANY)
    piece = jax.ShapeDtypeStruct((row_count, width // 2), LOW)
    ext = groups * TILE + WINDOW
    columns = 2 * width
    bits = places.bit_length() - 1
    count = 2 + 6 + 3 + 2 * bits + 2 * (tiles - 1)
    full = jnp.float32
    out_all, grad_all, sums = pl.pallas_call(
        functools.partial(body, half, groups, places, tiles, head_dim, scale, norm),
        out_shape=[piece, piece, jax.ShapeDtypeStruct((width, columns), LOW)],
        in_specs=[smem, anywhere, anywhere, vmem, vmem, vmem, vmem],
        out_specs=[anywhere, anywhere, vmem],
        scratch_shapes=[
            pltpu.VMEM((ext, width), LOW),
            pltpu.VMEM((ext, width), LOW),
            pltpu.VMEM((8, width // 2, width), LOW),
            pltpu.VMEM((3, width, width // 2), LOW),
            pltpu.VMEM((width // 2, width), LOW),
            pltpu.VMEM((TILE, TILE), LOW),
            pltpu.VMEM((TILE, TILE), LOW),
            pltpu.VMEM((ext, columns), LOW),
            pltpu.VMEM((ext, columns), LOW),
            pltpu.VMEM((2, width, columns), full),
            pltpu.VMEM((2, half, width // 2), LOW),
            pltpu.VMEM((2, half, width // 2), LOW),
            pltpu.VMEM((2, width, columns), full),
            pltpu.VMEM((2, width // 2, columns), full),
            pltpu.VMEM((2, width // 2, columns), full),
            pltpu.VMEM((width // 2, width), full),
            pltpu.VMEM((width // 4, width), full),
            pltpu.VMEM((width // 4, width), full),
            pltpu.VMEM((2, width // 4, width), full),
            pltpu.VMEM((width // 2, width), full),
            pltpu.VMEM((2, width // 4, width), full),
            pltpu.VMEM((width // 2, columns), full),
            pltpu.VMEM((width // 4, columns), full),
            pltpu.VMEM((tiles - 1, width >> bits, columns // tiles), full),
            pltpu.VMEM((width, columns), LOW),
            pltpu.SemaphoreType.DMA((2,)),
            pltpu.SemaphoreType.DMA((2,)),
            pltpu.SemaphoreType.DMA((count,)),
            pltpu.SemaphoreType.DMA((count,)),
        ],
        compiler_params=pltpu.CompilerParams(
            vmem_limit_bytes=56 * 1024 * 1024, collective_id=0, has_side_effects=True
        ),
    )(counts, nodes_in, cotangent, w_query, w_key, w_value, w_out)
    side = jax.ShapeDtypeStruct((width, width // 2), full)
    return pl.pallas_call(
        hand_over,
        out_shape=[piece, piece, side, side, side, jax.ShapeDtypeStruct((width // 2, width), full)],
        in_specs=[anywhere, anywhere, vmem],
        out_specs=[anywhere, anywhere] + [vmem] * 4,
        scratch_shapes=[pltpu.SemaphoreType.DMA((8,))],
        compiler_params=pltpu.CompilerParams(vmem_limit_bytes=16 * 1024 * 1024),
    )(out_all, grad_all, sums)


def solution(mesh):
    return jax.shard_map(
        per_device,
        mesh=mesh,
        in_specs=(
            P(("gz", "tile"), None),
            P(("gz", "tile"), None),
            P(None, "head"),
            P(None, "head"),
            P(None, "head"),
            P("head", None),
            P(),
        ),
        out_specs=(
            P(("gz", "tile"), "head"),
            P(("gz", "tile"), "head"),
            P(None, "head"),
            P(None, "head"),
            P(None, "head"),
            P("head", None),
        ),
        check_vma=False,
    )
```

```python
import functools
import math

import jax
import jax.numpy as jnp
from jax import lax
from jax.experimental import pallas as pl
from jax.experimental.pallas import tpu as pltpu
from jax.sharding import PartitionSpec as P

HEADS = 8
WINDOW = 128
DILATION = 4
TILE = WINDOW * DILATION
REACH = TILE // 2
LOW = jnp.bfloat16
NT = (((1,), (1,)), ((), ()))
MESH = pl.DeviceIdType.MESH


def dot(a, b, dims=(((1,), (0,)), ((), ()))):
    return lax.dot_general(a, b, dims, preferred_element_type=jnp.float32)


def block_mask(count_of, rows, width):
    parts = []
    iota = lax.broadcasted_iota(jnp.int32, (WINDOW, WINDOW), 0)
    for block in range(rows // WINDOW):
        kept = jnp.where(iota < count_of(block), 1.0, 0.0)
        parts.append(jnp.concatenate([kept] * (width // WINDOW), 1))
    return jnp.concatenate(parts, 0)


def window_grads(q, k, v, dc, qt, kt, vt, dct, mask, head_masks, scale, head_dim):
    heads = q.shape[1] // head_dim
    zeros = jnp.zeros((head_dim, WINDOW), LOW)

    def spread_t(array):
        blocks = []
        for h in range(heads):
            rows = [zeros] * heads
            rows[h] = array[h * head_dim : (h + 1) * head_dim]
            blocks.append(jnp.concatenate(rows, 0))
        return jnp.concatenate(blocks, 1)

    def spread(array):
        return jnp.concatenate([array * head_masks[h] for h in range(heads)], 0)

    deep = heads // 2

    def pair_dot(turned, array):
        rows = deep * head_dim
        gap = jnp.zeros((rows, WINDOW), LOW)
        left = jnp.concatenate([turned[:rows], gap], 0)
        right = jnp.concatenate([gap, turned[rows:]], 0)
        stacked = jnp.concatenate([array[:, : deep * WINDOW], array[:, deep * WINDOW :]], 0)
        product = dot(jnp.concatenate([left, right], 1), stacked)
        return jnp.concatenate(
            [
                product[
                    h * head_dim : (h + 1) * head_dim,
                    (h % deep) * WINDOW : (h % deep + 1) * WINDOW,
                ]
                for h in range(heads)
            ],
            0,
        )

    weights = jnp.exp2(dot(k, spread_t(qt)) * (scale * math.log2(math.e))) * mask
    attention = weights * (1.0 / jnp.sum(weights, axis=0, keepdims=True))
    attention_low = attention.astype(LOW)
    dattention = dot(v, spread_t(dct))
    center = jnp.sum(attention * dattention, axis=0, keepdims=True)
    dscores = (attention * (dattention - center)).astype(LOW)
    context = pair_dot(vt, attention_low).astype(LOW).T
    dq = (pair_dot(kt, dscores) * scale).astype(LOW).T
    dk = (dot(dscores, spread(q)) * scale).astype(LOW)
    dv = dot(attention_low, spread(dc)).astype(LOW)
    return jnp.concatenate([context, dq, dk, dv], 1)


def body(
    half, groups, places, tiles, head_dim, scale, norm,
    counts, nodes, cot, w_query, w_key, w_value, w_out,
    out_all, grad_all, sums,
    x_ext, c_ext, wt, w_peer, wo_peer, perm, perm_t, near, far, gw, mine_buf, peer_buf,
    head_masks, part, first, summed, head_a, head_b, later_a, later_b, sum_a, sum_b, held, later,
    tile_part, gathered, in_sems, own_sems, send_sems, recv_sems,
):
    gz, h, tile = lax.axis_index("gz"), lax.axis_index("head"), lax.axis_index("tile")
    position = gz * tiles + tile
    length = places * tiles
    first_block = (position * 2 + h) * (half // WINDOW) - REACH // WINDOW
    peer = {"head": 1 - h}
    bits = places.bit_length() - 1
    flags = [lax.rem(gz // (1 << k), 2) for k in range(bits)]
    partners = [{"gz": gz + (1 - 2 * flags[k]) * (1 << k)} for k in range(bits)]
    others = [{"tile": lax.rem(tile + d, tiles)} for d in range(1, tiles)]

    def along(distance):
        there = lax.rem(position + distance + length, length)
        return {"gz": there // tiles, "tile": lax.rem(there, tiles)}

    everyone = partners + [peer] + others + [along(1), along(-1)]
    barrier = pltpu.get_barrier_semaphore()
    for device in everyone:
        pl.semaphore_signal(barrier, inc=1, device_id=device, device_id_type=MESH)
    used = [2]

    def send(source, dest, device):
        slot = used[0]
        used[0] += 1
        copy = pltpu.make_async_remote_copy(
            src_ref=source, dst_ref=dest, send_sem=send_sems.at[slot],
            recv_sem=recv_sems.at[slot], device_id=device, device_id_type=MESH,
        )
        copy.start()
        return copy

    width = nodes.shape[1]
    total_blocks = counts.shape[0]
    local_rows = half + REACH
    copies = []
    for index, (source, dest) in enumerate(((nodes, x_ext), (cot, c_ext))):
        src = pl.ds(pl.multiple_of(h * (half - REACH), REACH), local_rows)
        dst = pl.ds(pl.multiple_of((1 - h) * REACH, REACH), local_rows)
        copies.append(pltpu.make_async_copy(source.at[src], dest.at[dst], in_sems.at[index]))
        copies[-1].start()
    pl.semaphore_wait(barrier, len(everyone))
    for index, source in enumerate((w_query, w_key, w_value)):
        copies.append(send(source, w_peer.at[index], peer))
    copies.append(send(w_out, wo_peer, peer))
    ahead = along(1 - 2 * h)
    edge_rows = pl.ds(pl.multiple_of((1 - h) * (2 * half - REACH), REACH), REACH)
    rim = pl.ds(pl.multiple_of(h * local_rows, REACH), REACH)
    for source, dest in ((nodes, x_ext), (cot, c_ext)):
        copies.append(send(source.at[edge_rows], dest.at[rim], ahead))

    def place_weight(kind, at, turned):
        for p in range(2):
            wt[kind, p * 128 + at : p * 128 + at + 64, :] = turned[p * 64 : (p + 1) * 64]

    for kind, source in enumerate((w_query, w_key, w_value)):
        place_weight(kind, 0, source[...].T)
    place_weight(3, 0, w_out[...])
    m = lax.broadcasted_iota(jnp.int32, (TILE, TILE), 0)
    n = lax.broadcasted_iota(jnp.int32, (TILE, TILE), 1)
    perm[...] = jnp.where(n == DILATION * (m % WINDOW) + m // WINDOW, 1.0, 0.0).astype(LOW)
    perm_t[...] = jnp.where(m == DILATION * (n % WINDOW) + n // WINDOW, 1.0, 0.0).astype(LOW)
    gw[...] = jnp.zeros_like(gw)
    lane = lax.broadcasted_iota(jnp.int32, (WINDOW, WINDOW), 1)
    for index in range(head_masks.shape[0]):
        inside = jnp.logical_and(lane >= index * head_dim, lane < (index + 1) * head_dim)
        head_masks[index] = jnp.where(inside, 1.0, 0.0).astype(LOW)
    tail = groups * TILE
    x_ext[tail:, :] = jnp.zeros((x_ext.shape[0] - tail, width), LOW)
    c_ext[tail:, :] = jnp.zeros((c_ext.shape[0] - tail, width), LOW)
    for copy in copies:
        copy.wait()
    for kind in range(3):
        place_weight(kind, 64, w_peer[kind].T)
    place_weight(3, 64, wo_peer[...])

    def count_at(block):
        return counts[lax.rem(first_block + block + total_blocks, total_blocks)]

    def project(x, c, part):
        own = slice(part * 128, (part + 1) * 128)
        triple = jnp.concatenate([wt[kind, own, :] for kind in range(3)], 0)
        single = wt[3, own, :]
        rows = dot(x, triple, NT).astype(LOW)
        columns = dot(triple, x, NT).astype(LOW)
        natural = [rows[:, kind * 128 : (kind + 1) * 128] for kind in range(3)]
        turned = [columns[kind * 128 : (kind + 1) * 128] for kind in range(3)]
        natural.append(dot(c, single, NT).astype(LOW))
        turned.append(dot(single, c, NT).astype(LOW))
        return natural, turned

    def windows(natural, turned, masks, store):
        for w in range(DILATION):
            rows = slice(w * WINDOW, (w + 1) * WINDOW)
            store(
                w,
                window_grads(
                    *[a[rows] for a in natural], *[a[:, rows] for a in turned],
                    masks[w], head_masks, scale, head_dim,
                ),
            )

    iota = lax.broadcasted_iota(jnp.int32, (WINDOW, WINDOW), 0)

    def attend(g):
        base = pl.multiple_of(g * TILE, TILE)
        block = g * DILATION
        c0 = [count_at(block + b) for b in range(DILATION + 1)]
        cot_mask = block_mask(lambda b: c0[b], TILE, width)
        cot_tile = c_ext[pl.ds(base, TILE), :] * cot_mask.astype(LOW)
        edge = lax.broadcasted_iota(jnp.int32, (64, width), 0)
        after = c_ext[pl.ds(pl.multiple_of(base + TILE, TILE), 64), :].astype(jnp.float32)
        after = (after * jnp.where(edge < c0[DILATION], 1.0, 0.0)).astype(LOW)
        x_tile = x_ext[pl.ds(base, TILE), :]
        near_x = x_ext[pl.ds(pl.multiple_of(base + 64, 64), TILE), :]
        near_c = jnp.concatenate([cot_tile[64:], after], 0)
        masks = []
        for w in range(DILATION):
            kept = jnp.where(
                iota < 64,
                jnp.where(iota + 64 < c0[w], 1.0, 0.0),
                jnp.where(iota - 64 < c0[w + 1], 1.0, 0.0),
            )
            masks.append(jnp.concatenate([kept] * head_masks.shape[0], 1))

        def store_near(w, value):
            near[pl.ds(pl.multiple_of(base + 64 + w * WINDOW, 64), WINDOW), :] = value

        windows(*project(near_x, near_c, 0), masks, store_near)

        far_x = dot(perm[...], x_tile).astype(LOW)
        far_c = dot(perm[...], cot_tile).astype(LOW)
        span = WINDOW // DILATION
        limit = jnp.where(
            iota < 2 * span,
            jnp.where(iota < span, c0[0], c0[1]),
            jnp.where(iota < 3 * span, c0[2], c0[3]),
        )
        spot = DILATION * (iota % span)
        masks = [
            jnp.concatenate([jnp.where(spot + w < limit, 1.0, 0.0)] * head_masks.shape[0], 1)
            for w in range(DILATION)
        ]
        pieces = []
        windows(*project(far_x, far_c, 1), masks, lambda w, value: pieces.append(value))
        far[pl.ds(base, TILE), :] = dot(perm_t[...], jnp.concatenate(pieces, 0)).astype(LOW)

    def finish(t):
        base = pl.multiple_of(t * TILE + REACH, REACH)
        dest = pl.ds(pl.multiple_of(t * TILE, TILE), TILE)
        block = t * DILATION + REACH // WINDOW
        mask = block_mask(lambda b: count_at(block + b), TILE, width)
        x = x_ext[pl.ds(base, TILE), :]
        c = c_ext[pl.ds(base, TILE), :] * mask.astype(LOW)
        res = [near[pl.ds(base, TILE), :], far[pl.ds(base, TILE), :]]
        sides = [
            jnp.concatenate([res[p][:, kind * 128 : (kind + 1) * 128] for p in range(2)], 1)
            for kind in range(4)
        ]
        grads = jnp.concatenate(sides[1:], 1)
        out = dot(sides[0], wt[3]) * mask
        grad = dot(grads, wt[:3].reshape(3 * width, width))
        home = pl.ds(pl.multiple_of(h * half + t * TILE, TILE), TILE)
        for slot, (value, whole) in enumerate(((out, out_all), (grad, grad_all))):
            value = value.astype(LOW)
            left, right = value[:, :128], value[:, 128:]
            mine_buf[slot, dest, :] = jnp.where(h == 0, left, right)
            peer_buf[slot, dest, :] = jnp.where(h == 0, right, left)
            pltpu.make_async_copy(
                mine_buf.at[slot, dest], whole.at[home], own_sems.at[slot]
            ).start()
            pltpu.make_async_remote_copy(
                src_ref=peer_buf.at[slot, dest],
                dst_ref=whole.at[home],
                send_sem=send_sems.at[slot],
                recv_sem=recv_sems.at[slot],
                device_id={"head": 1 - h},
                device_id_type=MESH,
            ).start()
        gw[:, :width] += dot(c.T, sides[0])
        gw[:, width:] += dot(x.T, grads)

    def step(g, carry):
        attend(g)

        @pl.when(g > 0)
        def _():
            finish(g - 1)

        return carry

    lax.fori_loop(0, groups, step, 0)
    for owner, at in ((0, 0), (1, 64)):
        for slot, kind in enumerate((1, 2, 3, 0)):
            start = kind * width + at
            part[owner, :, slot * 128 : (slot + 1) * 128] = jnp.concatenate(
                [gw[:, start : start + 64], gw[:, start + 128 : start + 192]], 1
            )
    rows, columns = part.shape[1:]
    middle = columns // 2
    size = rows // 2

    def keep(k):
        return pl.ds(pl.multiple_of(flags[k] * size, size), size)

    def give(k):
        return pl.ds(pl.multiple_of((1 - flags[k]) * size, size), size)

    send(part.at[:, give(0)], first, partners[0]).wait()
    summed[...] = part[:, keep(0), :] + first[...]
    base = flags[0] * size
    size = size // 2
    copy_a = send(summed.at[1, :, pl.ds(0, middle)], head_a, peer)
    copy_b = send(summed.at[:, give(1), pl.ds(middle, middle)], later_b, partners[1])
    copy_a.wait()
    sum_a[...] = summed[0, :, :middle] + head_a[...]
    copy_a = send(sum_a.at[give(1)], later_a, partners[1])
    copy_b.wait()
    sum_b[...] = summed[:, keep(1), middle:] + later_b[...]
    copy_b = send(sum_b.at[1], head_b, peer)
    copy_a.wait()
    copy_b.wait()
    held[:size, :middle] = sum_a[keep(1), :] + later_a[...]
    held[:size, middle:] = sum_b[0] + head_b[...]
    base = base + flags[1] * size
    at = 0
    start = 0
    for k in range(2, bits):
        whole = size
        size = size // 2
        old = held.at[pl.ds(at, whole)]
        send(old.at[give(k)], later.at[pl.ds(start, size)], partners[k]).wait()
        at += whole
        held[at : at + size, :] = old[keep(k), :] + later[start : start + size, :]
        start += size
        base = base + flags[k] * size
    wide = columns // tiles

    def lanes(index):
        return pl.ds(pl.multiple_of(index * wide, wide), wide)

    current = held.at[pl.ds(at, size)]
    copies = [
        send(current.at[:, lanes(device["tile"])], tile_part.at[d], device)
        for d, device in enumerate(others)
    ]
    total = current[:, lanes(tile)]
    for d, copy in enumerate(copies):
        copy.wait()
        total = total + tile_part[d]
    mine = pl.ds(pl.multiple_of(base, size), size)
    gathered[mine, lanes(tile)] = (total * norm).astype(LOW)
    piece = gathered.at[mine, lanes(tile)]
    for copy in [send(piece, piece, device) for device in others]:
        copy.wait()
    for k in range(bits - 1, -1, -1):
        piece = gathered.at[pl.ds(pl.multiple_of(base, size), size)]
        send(piece, piece, partners[k]).wait()
        base = base - flags[k] * size
        size = size * 2
    sums[...] = gathered[...]
    own_home = pl.ds(pl.multiple_of(h * half, TILE), half)
    peer_home = pl.ds(pl.multiple_of((1 - h) * half, TILE), half)
    for slot, whole in ((0, out_all), (1, grad_all)):
        pltpu.make_async_copy(mine_buf.at[slot], whole.at[own_home], own_sems.at[slot]).wait()
        sent = pltpu.make_async_remote_copy(
            src_ref=peer_buf.at[slot],
            dst_ref=whole.at[own_home],
            send_sem=send_sems.at[slot],
            recv_sem=recv_sems.at[slot],
            device_id={"head": 1 - h},
            device_id_type=MESH,
        )
        sent.wait_send()
        came = pltpu.make_async_remote_copy(
            src_ref=peer_buf.at[slot],
            dst_ref=whole.at[peer_home],
            send_sem=send_sems.at[slot],
            recv_sem=recv_sems.at[slot],
            device_id={"head": 1 - h},
            device_id_type=MESH,
        )
        came.wait_recv()


def hand_over(out_all, grad_all, sums, output, grad_nodes, *rest):
    grads, sems = rest[:4], rest[4]
    chunks = 4
    step = out_all.shape[0] // chunks
    copies = []
    for source, dest in ((out_all, output), (grad_all, grad_nodes)):
        for chunk in range(chunks):
            rows = pl.ds(chunk * step, step)
            copies.append(
                pltpu.make_async_copy(source.at[rows], dest.at[rows], sems.at[len(copies)])
            )
            copies[-1].start()
    result = sums[...].astype(jnp.float32)
    quarter = result.shape[1] // 4
    for slot in range(3):
        grads[slot][...] = result[:, slot * quarter : (slot + 1) * quarter]
    grads[3][...] = result[:, 3 * quarter :].T
    for copy in copies:
        copy.wait()


def per_device(nodes_in, cotangent, w_query, w_key, w_value, w_out, counts):
    row_count, width = nodes_in.shape
    half = row_count // 2
    head_dim = width // HEADS
    scale = head_dim ** (-0.5)
    places, tiles = lax.axis_size("gz"), lax.axis_size("tile")
    norm = float(row_count * places * tiles) ** (-0.5)
    groups = half // TILE + 1
    vmem = pl.BlockSpec(memory_space=pltpu.VMEM)
    smem = pl.BlockSpec(memory_space=pltpu.SMEM)
    anywhere = pl.BlockSpec(memory_space=pl.ANY)
    piece = jax.ShapeDtypeStruct((row_count, width // 2), LOW)
    ext = groups * TILE + WINDOW
    columns = 2 * width
    bits = places.bit_length() - 1
    count = 2 + 6 + 3 + 2 * bits + 2 * (tiles - 1)
    full = jnp.float32
    out_all, grad_all, sums = pl.pallas_call(
        functools.partial(body, half, groups, places, tiles, head_dim, scale, norm),
        out_shape=[piece, piece, jax.ShapeDtypeStruct((width, columns), LOW)],
        in_specs=[smem, anywhere, anywhere, vmem, vmem, vmem, vmem],
        out_specs=[anywhere, anywhere, vmem],
        scratch_shapes=[
            pltpu.VMEM((ext, width), LOW),
            pltpu.VMEM((ext, width), LOW),
            pltpu.VMEM((4, width, width), LOW),
            pltpu.VMEM((3, width, width // 2), LOW),
            pltpu.VMEM((width // 2, width), LOW),
            pltpu.VMEM((TILE, TILE), LOW),
            pltpu.VMEM((TILE, TILE), LOW),
            pltpu.VMEM((ext, columns), LOW),
            pltpu.VMEM((ext, columns), LOW),
            pltpu.VMEM((width, 2 * columns), full),
            pltpu.VMEM((2, half, width // 2), LOW),
            pltpu.VMEM((2, half, width // 2), LOW),
            pltpu.VMEM((HEADS // 2, WINDOW, WINDOW), LOW),
            pltpu.VMEM((2, width, columns), full),
            pltpu.VMEM((2, width // 2, columns), full),
            pltpu.VMEM((2, width // 2, columns), full),
            pltpu.VMEM((width // 2, width), full),
            pltpu.VMEM((width // 4, width), full),
            pltpu.VMEM((width // 4, width), full),
            pltpu.VMEM((2, width // 4, width), full),
            pltpu.VMEM((width // 2, width), full),
            pltpu.VMEM((2, width // 4, width), full),
            pltpu.VMEM((width // 2, columns), full),
            pltpu.VMEM((width // 4, columns), full),
            pltpu.VMEM((tiles - 1, width >> bits, columns // tiles), full),
            pltpu.VMEM((width, columns), LOW),
            pltpu.SemaphoreType.DMA((2,)),
            pltpu.SemaphoreType.DMA((2,)),
            pltpu.SemaphoreType.DMA((count,)),
            pltpu.SemaphoreType.DMA((count,)),
        ],
        compiler_params=pltpu.CompilerParams(
            vmem_limit_bytes=56 * 1024 * 1024, collective_id=0, has_side_effects=True
        ),
    )(counts, nodes_in, cotangent, w_query, w_key, w_value, w_out)
    side = jax.ShapeDtypeStruct((width, width // 2), full)
    return pl.pallas_call(
        hand_over,
        out_shape=[piece, piece, side, side, side, jax.ShapeDtypeStruct((width // 2, width), full)],
        in_specs=[anywhere, anywhere, vmem],
        out_specs=[anywhere, anywhere] + [vmem] * 4,
        scratch_shapes=[pltpu.SemaphoreType.DMA((8,))],
        compiler_params=pltpu.CompilerParams(vmem_limit_bytes=56 * 1024 * 1024),
    )(out_all, grad_all, sums)


def solution(mesh):
    return jax.shard_map(
        per_device,
        mesh=mesh,
        in_specs=(
            P(("gz", "tile"), None),
            P(("gz", "tile"), None),
            P(None, "head"),
            P(None, "head"),
            P(None, "head"),
            P("head", None),
            P(),
        ),
        out_specs=(
            P(("gz", "tile"), "head"),
            P(("gz", "tile"), "head"),
            P(None, "head"),
            P(None, "head"),
            P(None, "head"),
            P("head", None),
        ),
        check_vma=False,
    )
```

```python
import functools
import math

import jax
import jax.numpy as jnp
from jax import lax
from jax.experimental import pallas as pl
from jax.experimental.pallas import tpu as pltpu
from jax.sharding import PartitionSpec as P

HEADS = 8
WINDOW = 128
DILATION = 4
TILE = WINDOW * DILATION
REACH = TILE // 2
LOW = jnp.bfloat16
NT = (((1,), (1,)), ((), ()))
MESH = pl.DeviceIdType.MESH


def dot(a, b, dims=(((1,), (0,)), ((), ()))):
    return lax.dot_general(a, b, dims, preferred_element_type=jnp.float32)


def block_mask(count_of, rows, width):
    parts = []
    iota = lax.broadcasted_iota(jnp.int32, (WINDOW, WINDOW), 0)
    for block in range(rows // WINDOW):
        kept = jnp.where(iota < count_of(block), 1.0, 0.0)
        parts.append(jnp.concatenate([kept] * (width // WINDOW), 1))
    return jnp.concatenate(parts, 0)


def window_scores(k, v, qt, dct, head_dim):
    heads = k.shape[1] // head_dim
    zeros = jnp.zeros((head_dim, WINDOW), LOW)

    def spread_t(array):
        blocks = []
        for h in range(heads):
            rows = [zeros] * heads
            rows[h] = array[h * head_dim : (h + 1) * head_dim]
            blocks.append(jnp.concatenate(rows, 0))
        return jnp.concatenate(blocks, 1)

    return dot(k, spread_t(qt)), dot(v, spread_t(dct))


def window_grads(scores, dattention, q, dc, kt, vt, mask, head_masks, scale, head_dim):
    heads = q.shape[1] // head_dim

    def spread(array):
        return jnp.concatenate([array * head_masks[h] for h in range(heads)], 0)

    deep = heads // 2

    def pair_dot(turned, array):
        rows = deep * head_dim
        gap = jnp.zeros((rows, WINDOW), LOW)
        left = jnp.concatenate([turned[:rows], gap], 0)
        right = jnp.concatenate([gap, turned[rows:]], 0)
        stacked = jnp.concatenate([array[:, : deep * WINDOW], array[:, deep * WINDOW :]], 0)
        product = dot(jnp.concatenate([left, right], 1), stacked)
        return jnp.concatenate(
            [
                product[
                    h * head_dim : (h + 1) * head_dim,
                    (h % deep) * WINDOW : (h % deep + 1) * WINDOW,
                ]
                for h in range(heads)
            ],
            0,
        )

    weights = jnp.exp2(scores * (scale * math.log2(math.e))) * mask
    attention = weights * (1.0 / jnp.sum(weights, axis=0, keepdims=True))
    attention_low = attention.astype(LOW)
    center = jnp.sum(attention * dattention, axis=0, keepdims=True)
    dscores = (attention * (dattention - center)).astype(LOW)
    context = pair_dot(vt, attention_low).astype(LOW).T
    dq = (pair_dot(kt, dscores) * scale).astype(LOW).T
    dk = (dot(dscores, spread(q)) * scale).astype(LOW)
    dv = dot(attention_low, spread(dc)).astype(LOW)
    return jnp.concatenate([context, dq, dk, dv], 1)


def body(
    half, groups, places, tiles, head_dim, scale, norm,
    counts, nodes, cot, w_query, w_key, w_value, w_out,
    out_all, grad_all, sums,
    x_ext, c_ext, wt, w_peer, wo_peer, perm, perm_t, near, far, gw, mine_buf, peer_buf,
    head_masks, part, first, summed, head_a, head_b, later_a, later_b, sum_a, sum_b, held, later,
    tile_part, gathered, in_sems, own_sems, send_sems, recv_sems,
):
    gz, h, tile = lax.axis_index("gz"), lax.axis_index("head"), lax.axis_index("tile")
    position = gz * tiles + tile
    length = places * tiles
    first_block = (position * 2 + h) * (half // WINDOW) - REACH // WINDOW
    peer = {"head": 1 - h}
    bits = places.bit_length() - 1
    flags = [lax.rem(gz // (1 << k), 2) for k in range(bits)]
    partners = [{"gz": gz + (1 - 2 * flags[k]) * (1 << k)} for k in range(bits)]
    others = [{"tile": lax.rem(tile + d, tiles)} for d in range(1, tiles)]

    def along(distance):
        there = lax.rem(position + distance + length, length)
        return {"gz": there // tiles, "tile": lax.rem(there, tiles)}

    everyone = partners + [peer] + others + [along(1), along(-1)]
    barrier = pltpu.get_barrier_semaphore()
    for device in everyone:
        pl.semaphore_signal(barrier, inc=1, device_id=device, device_id_type=MESH)
    used = [2]

    def send(source, dest, device):
        slot = used[0]
        used[0] += 1
        copy = pltpu.make_async_remote_copy(
            src_ref=source, dst_ref=dest, send_sem=send_sems.at[slot],
            recv_sem=recv_sems.at[slot], device_id=device, device_id_type=MESH,
        )
        copy.start()
        return copy

    width = nodes.shape[1]
    total_blocks = counts.shape[0]
    local_rows = half + REACH
    copies = []
    for index, (source, dest) in enumerate(((nodes, x_ext), (cot, c_ext))):
        src = pl.ds(pl.multiple_of(h * (half - REACH), REACH), local_rows)
        dst = pl.ds(pl.multiple_of((1 - h) * REACH, REACH), local_rows)
        copies.append(pltpu.make_async_copy(source.at[src], dest.at[dst], in_sems.at[index]))
        copies[-1].start()
    pl.semaphore_wait(barrier, len(everyone))
    for index, source in enumerate((w_query, w_key, w_value)):
        copies.append(send(source, w_peer.at[index], peer))
    copies.append(send(w_out, wo_peer, peer))
    ahead = along(1 - 2 * h)
    edge_rows = pl.ds(pl.multiple_of((1 - h) * (2 * half - REACH), REACH), REACH)
    rim = pl.ds(pl.multiple_of(h * local_rows, REACH), REACH)
    for source, dest in ((nodes, x_ext), (cot, c_ext)):
        copies.append(send(source.at[edge_rows], dest.at[rim], ahead))

    def place_weight(kind, at, turned):
        for p in range(2):
            wt[kind, p * 128 + at : p * 128 + at + 64, :] = turned[p * 64 : (p + 1) * 64]

    for kind, source in enumerate((w_query, w_key, w_value)):
        place_weight(kind, 0, source[...].T)
    place_weight(3, 0, w_out[...])
    m = lax.broadcasted_iota(jnp.int32, (TILE, TILE), 0)
    n = lax.broadcasted_iota(jnp.int32, (TILE, TILE), 1)
    perm[...] = jnp.where(n == DILATION * (m % WINDOW) + m // WINDOW, 1.0, 0.0).astype(LOW)
    perm_t[...] = jnp.where(m == DILATION * (n % WINDOW) + n // WINDOW, 1.0, 0.0).astype(LOW)
    gw[...] = jnp.zeros_like(gw)
    lane = lax.broadcasted_iota(jnp.int32, (WINDOW, WINDOW), 1)
    for index in range(head_masks.shape[0]):
        inside = jnp.logical_and(lane >= index * head_dim, lane < (index + 1) * head_dim)
        head_masks[index] = jnp.where(inside, 1.0, 0.0).astype(LOW)
    tail = groups * TILE
    x_ext[tail:, :] = jnp.zeros((x_ext.shape[0] - tail, width), LOW)
    c_ext[tail:, :] = jnp.zeros((c_ext.shape[0] - tail, width), LOW)
    for copy in copies:
        copy.wait()
    for kind in range(3):
        place_weight(kind, 64, w_peer[kind].T)
    place_weight(3, 64, wo_peer[...])

    def count_at(block):
        return counts[lax.rem(first_block + block + total_blocks, total_blocks)]

    def project(x, c, part):
        own = slice(part * 128, (part + 1) * 128)
        triple = jnp.concatenate([wt[kind, own, :] for kind in range(3)], 0)
        single = wt[3, own, :]
        rows = dot(x, triple, NT).astype(LOW)
        columns = dot(triple, x, NT).astype(LOW)
        natural = [rows[:, kind * 128 : (kind + 1) * 128] for kind in range(3)]
        turned = [columns[kind * 128 : (kind + 1) * 128] for kind in range(3)]
        natural.append(dot(c, single, NT).astype(LOW))
        turned.append(dot(single, c, NT).astype(LOW))
        return natural, turned

    def windows(jobs):
        def rows(w):
            return slice(w * WINDOW, (w + 1) * WINDOW)

        def scores_of(job):
            natural, turned, _, w, _ = job
            at = rows(w)
            return window_scores(
                natural[1][at], natural[2][at], turned[0][:, at], turned[3][:, at], head_dim
            )

        ready = scores_of(jobs[0])
        for index, (natural, turned, mask, w, store) in enumerate(jobs):
            scores, dattention = ready
            if index + 1 < len(jobs):
                ready = scores_of(jobs[index + 1])
            at = rows(w)
            store(
                w,
                window_grads(
                    scores, dattention, natural[0][at], natural[3][at],
                    turned[1][:, at], turned[2][:, at], mask, head_masks, scale, head_dim,
                ),
            )

    iota = lax.broadcasted_iota(jnp.int32, (WINDOW, WINDOW), 0)

    def attend(g):
        base = pl.multiple_of(g * TILE, TILE)
        block = g * DILATION
        c0 = [count_at(block + b) for b in range(DILATION + 1)]
        cot_mask = block_mask(lambda b: c0[b], TILE, width)
        cot_tile = c_ext[pl.ds(base, TILE), :] * cot_mask.astype(LOW)
        edge = lax.broadcasted_iota(jnp.int32, (64, width), 0)
        after = c_ext[pl.ds(pl.multiple_of(base + TILE, TILE), 64), :].astype(jnp.float32)
        after = (after * jnp.where(edge < c0[DILATION], 1.0, 0.0)).astype(LOW)
        x_tile = x_ext[pl.ds(base, TILE), :]
        near_x = x_ext[pl.ds(pl.multiple_of(base + 64, 64), TILE), :]
        near_c = jnp.concatenate([cot_tile[64:], after], 0)
        masks = []
        for w in range(DILATION):
            kept = jnp.where(
                iota < 64,
                jnp.where(iota + 64 < c0[w], 1.0, 0.0),
                jnp.where(iota - 64 < c0[w + 1], 1.0, 0.0),
            )
            masks.append(jnp.concatenate([kept] * head_masks.shape[0], 1))

        def store_near(w, value):
            near[pl.ds(pl.multiple_of(base + 64 + w * WINDOW, 64), WINDOW), :] = value

        near_masks = masks

        far_x = dot(perm[...], x_tile).astype(LOW)
        far_c = dot(perm[...], cot_tile).astype(LOW)
        span = WINDOW // DILATION
        limit = jnp.where(
            iota < 2 * span,
            jnp.where(iota < span, c0[0], c0[1]),
            jnp.where(iota < 3 * span, c0[2], c0[3]),
        )
        spot = DILATION * (iota % span)
        masks = [
            jnp.concatenate([jnp.where(spot + w < limit, 1.0, 0.0)] * head_masks.shape[0], 1)
            for w in range(DILATION)
        ]
        pieces = []
        near_sides = project(near_x, near_c, 0)
        far_sides = project(far_x, far_c, 1)

        def store_far(w, value):
            pieces.append(value)

        jobs = [(*far_sides, masks[w], w, store_far) for w in range(DILATION)]
        jobs += [(*near_sides, near_masks[w], w, store_near) for w in range(DILATION)]
        windows(jobs)
        far[pl.ds(base, TILE), :] = dot(perm_t[...], jnp.concatenate(pieces, 0)).astype(LOW)

    def finish(t):
        base = pl.multiple_of(t * TILE + REACH, REACH)
        dest = pl.ds(pl.multiple_of(t * TILE, TILE), TILE)
        block = t * DILATION + REACH // WINDOW
        mask = block_mask(lambda b: count_at(block + b), TILE, width)
        x = x_ext[pl.ds(base, TILE), :]
        c = c_ext[pl.ds(base, TILE), :] * mask.astype(LOW)
        res = [near[pl.ds(base, TILE), :], far[pl.ds(base, TILE), :]]
        sides = [
            jnp.concatenate([res[p][:, kind * 128 : (kind + 1) * 128] for p in range(2)], 1)
            for kind in range(4)
        ]
        grads = jnp.concatenate(sides[1:], 1)
        out = dot(sides[0], wt[3]) * mask
        grad = dot(grads, wt[:3].reshape(3 * width, width))
        home = pl.ds(pl.multiple_of(h * half + t * TILE, TILE), TILE)
        for slot, (value, whole) in enumerate(((out, out_all), (grad, grad_all))):
            value = value.astype(LOW)
            left, right = value[:, :128], value[:, 128:]
            mine_buf[slot, dest, :] = jnp.where(h == 0, left, right)
            peer_buf[slot, dest, :] = jnp.where(h == 0, right, left)
            pltpu.make_async_copy(
                mine_buf.at[slot, dest], whole.at[home], own_sems.at[slot]
            ).start()
            pltpu.make_async_remote_copy(
                src_ref=peer_buf.at[slot, dest],
                dst_ref=whole.at[home],
                send_sem=send_sems.at[slot],
                recv_sem=recv_sems.at[slot],
                device_id={"head": 1 - h},
                device_id_type=MESH,
            ).start()
        gw[:, :width] += dot(c.T, sides[0])
        gw[:, width:] += dot(x.T, grads)

    def step(g, carry):
        attend(g)

        @pl.when(g > 0)
        def _():
            finish(g - 1)

        return carry

    lax.fori_loop(0, groups, step, 0)
    for owner, at in ((0, 0), (1, 64)):
        for slot, kind in enumerate((1, 2, 3, 0)):
            start = kind * width + at
            part[owner, :, slot * 128 : (slot + 1) * 128] = jnp.concatenate(
                [gw[:, start : start + 64], gw[:, start + 128 : start + 192]], 1
            )
    rows, columns = part.shape[1:]
    middle = columns // 2
    size = rows // 2

    def keep(k):
        return pl.ds(pl.multiple_of(flags[k] * size, size), size)

    def give(k):
        return pl.ds(pl.multiple_of((1 - flags[k]) * size, size), size)

    send(part.at[:, give(0)], first, partners[0]).wait()
    summed[...] = part[:, keep(0), :] + first[...]
    base = flags[0] * size
    size = size // 2
    copy_a = send(summed.at[1, :, pl.ds(0, middle)], head_a, peer)
    copy_b = send(summed.at[:, give(1), pl.ds(middle, middle)], later_b, partners[1])
    copy_a.wait()
    sum_a[...] = summed[0, :, :middle] + head_a[...]
    copy_a = send(sum_a.at[give(1)], later_a, partners[1])
    copy_b.wait()
    sum_b[...] = summed[:, keep(1), middle:] + later_b[...]
    copy_b = send(sum_b.at[1], head_b, peer)
    copy_a.wait()
    copy_b.wait()
    held[:size, :middle] = sum_a[keep(1), :] + later_a[...]
    held[:size, middle:] = sum_b[0] + head_b[...]
    base = base + flags[1] * size
    at = 0
    start = 0
    for k in range(2, bits):
        whole = size
        size = size // 2
        old = held.at[pl.ds(at, whole)]
        send(old.at[give(k)], later.at[pl.ds(start, size)], partners[k]).wait()
        at += whole
        held[at : at + size, :] = old[keep(k), :] + later[start : start + size, :]
        start += size
        base = base + flags[k] * size
    wide = columns // tiles

    def lanes(index):
        return pl.ds(pl.multiple_of(index * wide, wide), wide)

    current = held.at[pl.ds(at, size)]
    copies = [
        send(current.at[:, lanes(device["tile"])], tile_part.at[d], device)
        for d, device in enumerate(others)
    ]
    total = current[:, lanes(tile)]
    for d, copy in enumerate(copies):
        copy.wait()
        total = total + tile_part[d]
    mine = pl.ds(pl.multiple_of(base, size), size)
    gathered[mine, lanes(tile)] = (total * norm).astype(LOW)
    piece = gathered.at[mine, lanes(tile)]
    for copy in [send(piece, piece, device) for device in others]:
        copy.wait()
    for k in range(bits - 1, -1, -1):
        piece = gathered.at[pl.ds(pl.multiple_of(base, size), size)]
        send(piece, piece, partners[k]).wait()
        base = base - flags[k] * size
        size = size * 2
    sums[...] = gathered[...]
    own_home = pl.ds(pl.multiple_of(h * half, TILE), half)
    peer_home = pl.ds(pl.multiple_of((1 - h) * half, TILE), half)
    for slot, whole in ((0, out_all), (1, grad_all)):
        pltpu.make_async_copy(mine_buf.at[slot], whole.at[own_home], own_sems.at[slot]).wait()
        sent = pltpu.make_async_remote_copy(
            src_ref=peer_buf.at[slot],
            dst_ref=whole.at[own_home],
            send_sem=send_sems.at[slot],
            recv_sem=recv_sems.at[slot],
            device_id={"head": 1 - h},
            device_id_type=MESH,
        )
        sent.wait_send()
        came = pltpu.make_async_remote_copy(
            src_ref=peer_buf.at[slot],
            dst_ref=whole.at[peer_home],
            send_sem=send_sems.at[slot],
            recv_sem=recv_sems.at[slot],
            device_id={"head": 1 - h},
            device_id_type=MESH,
        )
        came.wait_recv()


def hand_over(out_all, grad_all, sums, output, grad_nodes, *rest):
    grads, (held, in_sems, out_sems) = rest[:4], rest[4:]
    chunks = in_sems.shape[1]
    step = out_all.shape[0] // chunks
    arrays = ((out_all, output), (grad_all, grad_nodes))

    def copy_in(slot, chunk):
        rows = pl.ds(chunk * step, step)
        return pltpu.make_async_copy(
            arrays[slot][0].at[rows], held.at[slot, rows], in_sems.at[slot, chunk]
        )

    def copy_out(slot, chunk):
        rows = pl.ds(chunk * step, step)
        return pltpu.make_async_copy(
            held.at[slot, rows], arrays[slot][1].at[rows], out_sems.at[slot, chunk]
        )

    order = [(slot, chunk) for chunk in range(chunks) for slot in range(2)]
    for spot in order:
        copy_in(*spot).start()
    result = sums[...].astype(jnp.float32)
    quarter = result.shape[1] // 4
    for slot in range(3):
        grads[slot][...] = result[:, slot * quarter : (slot + 1) * quarter]
    grads[3][...] = result[:, 3 * quarter :].T
    for spot in order:
        copy_in(*spot).wait()
        copy_out(*spot).start()
    for spot in order:
        copy_out(*spot).wait()


def per_device(nodes_in, cotangent, w_query, w_key, w_value, w_out, counts):
    row_count, width = nodes_in.shape
    half = row_count // 2
    head_dim = width // HEADS
    scale = head_dim ** (-0.5)
    places, tiles = lax.axis_size("gz"), lax.axis_size("tile")
    norm = float(row_count * places * tiles) ** (-0.5)
    groups = half // TILE + 1
    vmem = pl.BlockSpec(memory_space=pltpu.VMEM)
    smem = pl.BlockSpec(memory_space=pltpu.SMEM)
    anywhere = pl.BlockSpec(memory_space=pl.ANY)
    piece = jax.ShapeDtypeStruct((row_count, width // 2), LOW)
    ext = groups * TILE + WINDOW
    columns = 2 * width
    bits = places.bit_length() - 1
    count = 2 + 6 + 3 + 2 * bits + 2 * (tiles - 1)
    full = jnp.float32
    out_all, grad_all, sums = pl.pallas_call(
        functools.partial(body, half, groups, places, tiles, head_dim, scale, norm),
        out_shape=[piece, piece, jax.ShapeDtypeStruct((width, columns), LOW)],
        in_specs=[smem, anywhere, anywhere, vmem, vmem, vmem, vmem],
        out_specs=[anywhere, anywhere, vmem],
        scratch_shapes=[
            pltpu.VMEM((ext, width), LOW),
            pltpu.VMEM((ext, width), LOW),
            pltpu.VMEM((4, width, width), LOW),
            pltpu.VMEM((3, width, width // 2), LOW),
            pltpu.VMEM((width // 2, width), LOW),
            pltpu.VMEM((TILE, TILE), LOW),
            pltpu.VMEM((TILE, TILE), LOW),
            pltpu.VMEM((ext, columns), LOW),
            pltpu.VMEM((ext, columns), LOW),
            pltpu.VMEM((width, 2 * columns), full),
            pltpu.VMEM((2, half, width // 2), LOW),
            pltpu.VMEM((2, half, width // 2), LOW),
            pltpu.VMEM((HEADS // 2, WINDOW, WINDOW), LOW),
            pltpu.VMEM((2, width, columns), full),
            pltpu.VMEM((2, width // 2, columns), full),
            pltpu.VMEM((2, width // 2, columns), full),
            pltpu.VMEM((width // 2, width), full),
            pltpu.VMEM((width // 4, width), full),
            pltpu.VMEM((width // 4, width), full),
            pltpu.VMEM((2, width // 4, width), full),
            pltpu.VMEM((width // 2, width), full),
            pltpu.VMEM((2, width // 4, width), full),
            pltpu.VMEM((width // 2, columns), full),
            pltpu.VMEM((width // 4, columns), full),
            pltpu.VMEM((tiles - 1, width >> bits, columns // tiles), full),
            pltpu.VMEM((width, columns), LOW),
            pltpu.SemaphoreType.DMA((2,)),
            pltpu.SemaphoreType.DMA((2,)),
            pltpu.SemaphoreType.DMA((count,)),
            pltpu.SemaphoreType.DMA((count,)),
        ],
        compiler_params=pltpu.CompilerParams(
            vmem_limit_bytes=56 * 1024 * 1024, collective_id=0, has_side_effects=True
        ),
    )(counts, nodes_in, cotangent, w_query, w_key, w_value, w_out)
    side = jax.ShapeDtypeStruct((width, width // 2), full)
    return pl.pallas_call(
        hand_over,
        out_shape=[piece, piece, side, side, side, jax.ShapeDtypeStruct((width // 2, width), full)],
        in_specs=[anywhere, anywhere, vmem],
        out_specs=[anywhere, anywhere] + [vmem] * 4,
        scratch_shapes=[
            pltpu.VMEM((2, row_count, width // 2), LOW),
            pltpu.SemaphoreType.DMA((2, 4)),
            pltpu.SemaphoreType.DMA((2, 4)),
        ],
        compiler_params=pltpu.CompilerParams(vmem_limit_bytes=56 * 1024 * 1024),
    )(out_all, grad_all, sums)


def solution(mesh):
    return jax.shard_map(
        per_device,
        mesh=mesh,
        in_specs=(
            P(("gz", "tile"), None),
            P(("gz", "tile"), None),
            P(None, "head"),
            P(None, "head"),
            P(None, "head"),
            P("head", None),
            P(),
        ),
        out_specs=(
            P(("gz", "tile"), "head"),
            P(("gz", "tile"), "head"),
            P(None, "head"),
            P(None, "head"),
            P(None, "head"),
            P("head", None),
        ),
        check_vma=False,
    )
```

```python
import functools
import math

import jax
import jax.numpy as jnp
from jax import lax
from jax.experimental import pallas as pl
from jax.experimental.pallas import tpu as pltpu
from jax.sharding import PartitionSpec as P

HEADS = 8
WINDOW = 128
DILATION = 4
TILE = WINDOW * DILATION
REACH = TILE // 2
LOW = jnp.bfloat16
NT = (((1,), (1,)), ((), ()))
MESH = pl.DeviceIdType.MESH


def dot(a, b, dims=(((1,), (0,)), ((), ()))):
    return lax.dot_general(a, b, dims, preferred_element_type=jnp.float32)


def block_mask(count_of, rows, width):
    parts = []
    iota = lax.broadcasted_iota(jnp.int32, (WINDOW, WINDOW), 0)
    for block in range(rows // WINDOW):
        kept = jnp.where(iota < count_of(block), 1.0, 0.0)
        parts.append(jnp.concatenate([kept] * (width // WINDOW), 1))
    return jnp.concatenate(parts, 0)


def window_scores(k, v, qt, dct, head_dim):
    heads = k.shape[1] // head_dim
    zeros = jnp.zeros((head_dim, WINDOW), LOW)

    def spread_t(array):
        blocks = []
        for h in range(heads):
            rows = [zeros] * heads
            rows[h] = array[h * head_dim : (h + 1) * head_dim]
            blocks.append(jnp.concatenate(rows, 0))
        return jnp.concatenate(blocks, 1)

    return dot(k, spread_t(qt)), dot(v, spread_t(dct))


def window_grads(scores, dattention, q, dc, kt, vt, mask, head_masks, scale, head_dim):
    heads = q.shape[1] // head_dim

    def spread(array):
        return jnp.concatenate([array * head_masks[h] for h in range(heads)], 0)

    deep = heads // 2

    def pair_dot(turned, array):
        rows = deep * head_dim
        gap = jnp.zeros((rows, WINDOW), LOW)
        left = jnp.concatenate([turned[:rows], gap], 0)
        right = jnp.concatenate([gap, turned[rows:]], 0)
        stacked = jnp.concatenate([array[:, : deep * WINDOW], array[:, deep * WINDOW :]], 0)
        product = dot(jnp.concatenate([left, right], 1), stacked)
        return jnp.concatenate(
            [
                product[
                    h * head_dim : (h + 1) * head_dim,
                    (h % deep) * WINDOW : (h % deep + 1) * WINDOW,
                ]
                for h in range(heads)
            ],
            0,
        )

    weights = jnp.exp2(scores * (scale * math.log2(math.e))) * mask
    attention = weights * (1.0 / jnp.sum(weights, axis=0, keepdims=True))
    attention_low = attention.astype(LOW)
    center = jnp.sum(attention * dattention, axis=0, keepdims=True)
    dscores = (attention * (dattention - center)).astype(LOW)
    context = pair_dot(vt, attention_low).astype(LOW).T
    dq = (pair_dot(kt, dscores) * scale).astype(LOW).T
    dk = (dot(dscores, spread(q)) * scale).astype(LOW)
    dv = dot(attention_low, spread(dc)).astype(LOW)
    return jnp.concatenate([context, dq, dk, dv], 1)


def body(
    half, groups, places, tiles, head_dim, scale, norm,
    counts, nodes, cot, w_query, w_key, w_value, w_out,
    out_all, grad_all, sums,
    x_ext, c_ext, wt, w_peer, wo_peer, perm, perm_t, near, far, gw, mine_buf, peer_buf,
    head_masks, part, first, summed, head_a, head_b, later_a, later_b, sum_a, sum_b, held, later,
    tile_part, gathered, in_sems, own_sems, send_sems, recv_sems,
):
    gz, h, tile = lax.axis_index("gz"), lax.axis_index("head"), lax.axis_index("tile")
    position = gz * tiles + tile
    length = places * tiles
    first_block = (position * 2 + h) * (half // WINDOW) - REACH // WINDOW
    peer = {"head": 1 - h}
    bits = places.bit_length() - 1
    flags = [lax.rem(gz // (1 << k), 2) for k in range(bits)]
    partners = [{"gz": gz + (1 - 2 * flags[k]) * (1 << k)} for k in range(bits)]
    others = [{"tile": lax.rem(tile + d, tiles)} for d in range(1, tiles)]

    def along(distance):
        there = lax.rem(position + distance + length, length)
        return {"gz": there // tiles, "tile": lax.rem(there, tiles)}

    everyone = partners + [peer] + others + [along(1), along(-1)]
    barrier = pltpu.get_barrier_semaphore()
    for device in everyone:
        pl.semaphore_signal(barrier, inc=1, device_id=device, device_id_type=MESH)
    used = [2]

    def send(source, dest, device):
        slot = used[0]
        used[0] += 1
        copy = pltpu.make_async_remote_copy(
            src_ref=source, dst_ref=dest, send_sem=send_sems.at[slot],
            recv_sem=recv_sems.at[slot], device_id=device, device_id_type=MESH,
        )
        copy.start()
        return copy

    width = nodes.shape[1]
    total_blocks = counts.shape[0]
    local_rows = half + REACH
    copies = []
    for index, (source, dest) in enumerate(((nodes, x_ext), (cot, c_ext))):
        src = pl.ds(pl.multiple_of(h * (half - REACH), REACH), local_rows)
        dst = pl.ds(pl.multiple_of((1 - h) * REACH, REACH), local_rows)
        copies.append(pltpu.make_async_copy(source.at[src], dest.at[dst], in_sems.at[index]))
        copies[-1].start()
    pl.semaphore_wait(barrier, len(everyone))
    for index, source in enumerate((w_query, w_key, w_value)):
        copies.append(send(source, w_peer.at[index], peer))
    copies.append(send(w_out, wo_peer, peer))
    ahead = along(1 - 2 * h)
    edge_rows = pl.ds(pl.multiple_of((1 - h) * (2 * half - REACH), REACH), REACH)
    rim = pl.ds(pl.multiple_of(h * local_rows, REACH), REACH)
    for source, dest in ((nodes, x_ext), (cot, c_ext)):
        copies.append(send(source.at[edge_rows], dest.at[rim], ahead))

    def place_weight(kind, at, turned):
        for p in range(2):
            wt[kind, p * 128 + at : p * 128 + at + 64, :] = turned[p * 64 : (p + 1) * 64]

    for kind, source in enumerate((w_query, w_key, w_value)):
        place_weight(kind, 0, source[...].T)
    place_weight(3, 0, w_out[...])
    m = lax.broadcasted_iota(jnp.int32, (TILE, TILE), 0)
    n = lax.broadcasted_iota(jnp.int32, (TILE, TILE), 1)
    perm[...] = jnp.where(n == DILATION * (m % WINDOW) + m // WINDOW, 1.0, 0.0).astype(LOW)
    perm_t[...] = jnp.where(m == DILATION * (n % WINDOW) + n // WINDOW, 1.0, 0.0).astype(LOW)
    gw[...] = jnp.zeros_like(gw)
    lane = lax.broadcasted_iota(jnp.int32, (WINDOW, WINDOW), 1)
    for index in range(head_masks.shape[0]):
        inside = jnp.logical_and(lane >= index * head_dim, lane < (index + 1) * head_dim)
        head_masks[index] = jnp.where(inside, 1.0, 0.0).astype(LOW)
    tail = groups * TILE
    x_ext[tail:, :] = jnp.zeros((x_ext.shape[0] - tail, width), LOW)
    c_ext[tail:, :] = jnp.zeros((c_ext.shape[0] - tail, width), LOW)
    for copy in copies:
        copy.wait()
    for kind in range(3):
        place_weight(kind, 64, w_peer[kind].T)
    place_weight(3, 64, wo_peer[...])

    def count_at(block):
        return counts[lax.rem(first_block + block + total_blocks, total_blocks)]

    def project(x, c, part):
        own = slice(part * 128, (part + 1) * 128)
        triple = jnp.concatenate([wt[kind, own, :] for kind in range(3)], 0)
        single = wt[3, own, :]
        rows = dot(x, triple, NT).astype(LOW)
        columns = dot(triple, x, NT).astype(LOW)
        natural = [rows[:, kind * 128 : (kind + 1) * 128] for kind in range(3)]
        turned = [columns[kind * 128 : (kind + 1) * 128] for kind in range(3)]
        natural.append(dot(c, single, NT).astype(LOW))
        turned.append(dot(single, c, NT).astype(LOW))
        return natural, turned

    def windows(jobs):
        def rows(w):
            return slice(w * WINDOW, (w + 1) * WINDOW)

        def scores_of(job):
            natural, turned, _, w, _ = job
            at = rows(w)
            return window_scores(
                natural[1][at], natural[2][at], turned[0][:, at], turned[3][:, at], head_dim
            )

        ready = scores_of(jobs[0])
        for index, (natural, turned, mask, w, store) in enumerate(jobs):
            scores, dattention = ready
            if index + 1 < len(jobs):
                ready = scores_of(jobs[index + 1])
            at = rows(w)
            store(
                w,
                window_grads(
                    scores, dattention, natural[0][at], natural[3][at],
                    turned[1][:, at], turned[2][:, at], mask, head_masks, scale, head_dim,
                ),
            )

    iota = lax.broadcasted_iota(jnp.int32, (WINDOW, WINDOW), 0)

    def attend(g):
        base = pl.multiple_of(g * TILE, TILE)
        block = g * DILATION
        c0 = [count_at(block + b) for b in range(DILATION + 1)]
        cot_mask = block_mask(lambda b: c0[b], TILE, width)
        cot_tile = c_ext[pl.ds(base, TILE), :] * cot_mask.astype(LOW)
        edge = lax.broadcasted_iota(jnp.int32, (64, width), 0)
        after = c_ext[pl.ds(pl.multiple_of(base + TILE, TILE), 64), :].astype(jnp.float32)
        after = (after * jnp.where(edge < c0[DILATION], 1.0, 0.0)).astype(LOW)
        x_tile = x_ext[pl.ds(base, TILE), :]
        near_x = x_ext[pl.ds(pl.multiple_of(base + 64, 64), TILE), :]
        near_c = jnp.concatenate([cot_tile[64:], after], 0)
        masks = []
        for w in range(DILATION):
            kept = jnp.where(
                iota < 64,
                jnp.where(iota + 64 < c0[w], 1.0, 0.0),
                jnp.where(iota - 64 < c0[w + 1], 1.0, 0.0),
            )
            masks.append(jnp.concatenate([kept] * head_masks.shape[0], 1))

        def store_near(w, value):
            near[pl.ds(pl.multiple_of(base + 64 + w * WINDOW, 64), WINDOW), :] = value

        near_masks = masks

        far_x = dot(perm[...], x_tile).astype(LOW)
        far_c = dot(perm[...], cot_tile).astype(LOW)
        span = WINDOW // DILATION
        limit = jnp.where(
            iota < 2 * span,
            jnp.where(iota < span, c0[0], c0[1]),
            jnp.where(iota < 3 * span, c0[2], c0[3]),
        )
        spot = DILATION * (iota % span)
        masks = [
            jnp.concatenate([jnp.where(spot + w < limit, 1.0, 0.0)] * head_masks.shape[0], 1)
            for w in range(DILATION)
        ]
        pieces = []
        near_sides = project(near_x, near_c, 0)
        far_sides = project(far_x, far_c, 1)

        def store_far(w, value):
            pieces.append(value)

        jobs = [(*far_sides, masks[w], w, store_far) for w in range(DILATION)]
        jobs += [(*near_sides, near_masks[w], w, store_near) for w in range(DILATION)]
        windows(jobs)
        far[pl.ds(base, TILE), :] = dot(perm_t[...], jnp.concatenate(pieces, 0)).astype(LOW)

    def finish(t):
        base = pl.multiple_of(t * TILE + REACH, REACH)
        dest = pl.ds(pl.multiple_of(t * TILE, TILE), TILE)
        block = t * DILATION + REACH // WINDOW
        mask = block_mask(lambda b: count_at(block + b), TILE, width)
        x = x_ext[pl.ds(base, TILE), :]
        c = c_ext[pl.ds(base, TILE), :] * mask.astype(LOW)
        res = [near[pl.ds(base, TILE), :], far[pl.ds(base, TILE), :]]
        sides = [
            jnp.concatenate([res[p][:, kind * 128 : (kind + 1) * 128] for p in range(2)], 1)
            for kind in range(4)
        ]
        grads = jnp.concatenate(sides[1:], 1)
        out = dot(sides[0], wt[3]) * mask
        grad = dot(grads, wt[:3].reshape(3 * width, width))
        home = pl.ds(pl.multiple_of(h * half + t * TILE, TILE), TILE)
        for slot, (value, whole) in enumerate(((out, out_all), (grad, grad_all))):
            value = value.astype(LOW)
            left, right = value[:, :128], value[:, 128:]
            mine_buf[slot, dest, :] = jnp.where(h == 0, left, right)
            peer_buf[slot, dest, :] = jnp.where(h == 0, right, left)
            pltpu.make_async_copy(
                mine_buf.at[slot, dest], whole.at[home], own_sems.at[slot]
            ).start()
            pltpu.make_async_remote_copy(
                src_ref=peer_buf.at[slot, dest],
                dst_ref=whole.at[home],
                send_sem=send_sems.at[slot],
                recv_sem=recv_sems.at[slot],
                device_id={"head": 1 - h},
                device_id_type=MESH,
            ).start()
        gw[:, :width] += dot(c.T, sides[0])
        gw[:, width:] += dot(x.T, grads)

    def begin(g, carry):
        attend(g)
        return carry

    def step(g, carry):
        finish(g - 2)
        attend(g)
        return carry

    lax.fori_loop(0, 2, begin, 0)
    lax.fori_loop(2, groups, step, 0)
    finish(groups - 2)
    for owner, at in ((0, 0), (1, 64)):
        for slot, kind in enumerate((1, 2, 3, 0)):
            start = kind * width + at
            part[owner, :, slot * 128 : (slot + 1) * 128] = jnp.concatenate(
                [gw[:, start : start + 64], gw[:, start + 128 : start + 192]], 1
            )
    rows, columns = part.shape[1:]
    middle = columns // 2
    size = rows // 2

    def keep(k):
        return pl.ds(pl.multiple_of(flags[k] * size, size), size)

    def give(k):
        return pl.ds(pl.multiple_of((1 - flags[k]) * size, size), size)

    send(part.at[:, give(0)], first, partners[0]).wait()
    summed[...] = part[:, keep(0), :] + first[...]
    base = flags[0] * size
    size = size // 2
    copy_a = send(summed.at[1, :, pl.ds(0, middle)], head_a, peer)
    copy_b = send(summed.at[:, give(1), pl.ds(middle, middle)], later_b, partners[1])
    copy_a.wait()
    sum_a[...] = summed[0, :, :middle] + head_a[...]
    copy_a = send(sum_a.at[give(1)], later_a, partners[1])
    copy_b.wait()
    sum_b[...] = summed[:, keep(1), middle:] + later_b[...]
    copy_b = send(sum_b.at[1], head_b, peer)
    copy_a.wait()
    copy_b.wait()
    held[:size, :middle] = sum_a[keep(1), :] + later_a[...]
    held[:size, middle:] = sum_b[0] + head_b[...]
    base = base + flags[1] * size
    at = 0
    start = 0
    for k in range(2, bits):
        whole = size
        size = size // 2
        old = held.at[pl.ds(at, whole)]
        send(old.at[give(k)], later.at[pl.ds(start, size)], partners[k]).wait()
        at += whole
        held[at : at + size, :] = old[keep(k), :] + later[start : start + size, :]
        start += size
        base = base + flags[k] * size
    wide = columns // tiles

    def lanes(index):
        return pl.ds(pl.multiple_of(index * wide, wide), wide)

    current = held.at[pl.ds(at, size)]
    copies = [
        send(current.at[:, lanes(device["tile"])], tile_part.at[d], device)
        for d, device in enumerate(others)
    ]
    total = current[:, lanes(tile)]
    for d, copy in enumerate(copies):
        copy.wait()
        total = total + tile_part[d]
    mine = pl.ds(pl.multiple_of(base, size), size)
    gathered[mine, lanes(tile)] = (total * norm).astype(LOW)
    piece = gathered.at[mine, lanes(tile)]
    for copy in [send(piece, piece, device) for device in others]:
        copy.wait()
    for k in range(bits - 1, -1, -1):
        piece = gathered.at[pl.ds(pl.multiple_of(base, size), size)]
        send(piece, piece, partners[k]).wait()
        base = base - flags[k] * size
        size = size * 2
    sums[...] = gathered[...]
    own_home = pl.ds(pl.multiple_of(h * half, TILE), half)
    peer_home = pl.ds(pl.multiple_of((1 - h) * half, TILE), half)
    for slot, whole in ((0, out_all), (1, grad_all)):
        pltpu.make_async_copy(mine_buf.at[slot], whole.at[own_home], own_sems.at[slot]).wait()
        sent = pltpu.make_async_remote_copy(
            src_ref=peer_buf.at[slot],
            dst_ref=whole.at[own_home],
            send_sem=send_sems.at[slot],
            recv_sem=recv_sems.at[slot],
            device_id={"head": 1 - h},
            device_id_type=MESH,
        )
        sent.wait_send()
        came = pltpu.make_async_remote_copy(
            src_ref=peer_buf.at[slot],
            dst_ref=whole.at[peer_home],
            send_sem=send_sems.at[slot],
            recv_sem=recv_sems.at[slot],
            device_id={"head": 1 - h},
            device_id_type=MESH,
        )
        came.wait_recv()


def hand_over(out_all, grad_all, sums, output, grad_nodes, *rest):
    grads, (held, in_sems, out_sems) = rest[:4], rest[4:]
    chunks = in_sems.shape[1]
    step = out_all.shape[0] // chunks
    arrays = ((out_all, output), (grad_all, grad_nodes))

    def copy_in(slot, chunk):
        rows = pl.ds(chunk * step, step)
        return pltpu.make_async_copy(
            arrays[slot][0].at[rows], held.at[slot, rows], in_sems.at[slot, chunk]
        )

    def copy_out(slot, chunk):
        rows = pl.ds(chunk * step, step)
        return pltpu.make_async_copy(
            held.at[slot, rows], arrays[slot][1].at[rows], out_sems.at[slot, chunk]
        )

    order = [(slot, chunk) for chunk in range(chunks) for slot in range(2)]
    for spot in order:
        copy_in(*spot).start()
    result = sums[...].astype(jnp.float32)
    quarter = result.shape[1] // 4
    for slot in range(3):
        grads[slot][...] = result[:, slot * quarter : (slot + 1) * quarter]
    grads[3][...] = result[:, 3 * quarter :].T
    for spot in order:
        copy_in(*spot).wait()
        copy_out(*spot).start()
    for spot in order:
        copy_out(*spot).wait()


def per_device(nodes_in, cotangent, w_query, w_key, w_value, w_out, counts):
    row_count, width = nodes_in.shape
    half = row_count // 2
    head_dim = width // HEADS
    scale = head_dim ** (-0.5)
    places, tiles = lax.axis_size("gz"), lax.axis_size("tile")
    norm = float(row_count * places * tiles) ** (-0.5)
    groups = half // TILE + 1
    vmem = pl.BlockSpec(memory_space=pltpu.VMEM)
    smem = pl.BlockSpec(memory_space=pltpu.SMEM)
    anywhere = pl.BlockSpec(memory_space=pl.ANY)
    piece = jax.ShapeDtypeStruct((row_count, width // 2), LOW)
    ext = groups * TILE + WINDOW
    columns = 2 * width
    bits = places.bit_length() - 1
    count = 2 + 6 + 3 + 2 * bits + 2 * (tiles - 1)
    full = jnp.float32
    out_all, grad_all, sums = pl.pallas_call(
        functools.partial(body, half, groups, places, tiles, head_dim, scale, norm),
        out_shape=[piece, piece, jax.ShapeDtypeStruct((width, columns), LOW)],
        in_specs=[smem, anywhere, anywhere, vmem, vmem, vmem, vmem],
        out_specs=[anywhere, anywhere, vmem],
        scratch_shapes=[
            pltpu.VMEM((ext, width), LOW),
            pltpu.VMEM((ext, width), LOW),
            pltpu.VMEM((4, width, width), LOW),
            pltpu.VMEM((3, width, width // 2), LOW),
            pltpu.VMEM((width // 2, width), LOW),
            pltpu.VMEM((TILE, TILE), LOW),
            pltpu.VMEM((TILE, TILE), LOW),
            pltpu.VMEM((ext, columns), LOW),
            pltpu.VMEM((ext, columns), LOW),
            pltpu.VMEM((width, 2 * columns), full),
            pltpu.VMEM((2, half, width // 2), LOW),
            pltpu.VMEM((2, half, width // 2), LOW),
            pltpu.VMEM((HEADS // 2, WINDOW, WINDOW), LOW),
            pltpu.VMEM((2, width, columns), full),
            pltpu.VMEM((2, width // 2, columns), full),
            pltpu.VMEM((2, width // 2, columns), full),
            pltpu.VMEM((width // 2, width), full),
            pltpu.VMEM((width // 4, width), full),
            pltpu.VMEM((width // 4, width), full),
            pltpu.VMEM((2, width // 4, width), full),
            pltpu.VMEM((width // 2, width), full),
            pltpu.VMEM((2, width // 4, width), full),
            pltpu.VMEM((width // 2, columns), full),
            pltpu.VMEM((width // 4, columns), full),
            pltpu.VMEM((tiles - 1, width >> bits, columns // tiles), full),
            pltpu.VMEM((width, columns), LOW),
            pltpu.SemaphoreType.DMA((2,)),
            pltpu.SemaphoreType.DMA((2,)),
            pltpu.SemaphoreType.DMA((count,)),
            pltpu.SemaphoreType.DMA((count,)),
        ],
        compiler_params=pltpu.CompilerParams(
            vmem_limit_bytes=56 * 1024 * 1024, collective_id=0, has_side_effects=True
        ),
    )(counts, nodes_in, cotangent, w_query, w_key, w_value, w_out)
    side = jax.ShapeDtypeStruct((width, width // 2), full)
    return pl.pallas_call(
        hand_over,
        out_shape=[piece, piece, side, side, side, jax.ShapeDtypeStruct((width // 2, width), full)],
        in_specs=[anywhere, anywhere, vmem],
        out_specs=[anywhere, anywhere] + [vmem] * 4,
        scratch_shapes=[
            pltpu.VMEM((2, row_count, width // 2), LOW),
            pltpu.SemaphoreType.DMA((2, 4)),
            pltpu.SemaphoreType.DMA((2, 4)),
        ],
        compiler_params=pltpu.CompilerParams(vmem_limit_bytes=56 * 1024 * 1024),
    )(out_all, grad_all, sums)


def solution(mesh):
    return jax.shard_map(
        per_device,
        mesh=mesh,
        in_specs=(
            P(("gz", "tile"), None),
            P(("gz", "tile"), None),
            P(None, "head"),
            P(None, "head"),
            P(None, "head"),
            P("head", None),
            P(),
        ),
        out_specs=(
            P(("gz", "tile"), "head"),
            P(("gz", "tile"), "head"),
            P(None, "head"),
            P(None, "head"),
            P(None, "head"),
            P("head", None),
        ),
        check_vma=False,
    )
```
